256 devices in a mesh: dp: 32 (over z, x_hi, core), tensor: 8 (over y, x_lo).
Axes of the slice: x: 4 (x_hi: 2, x_lo: 2; x = x_hi * 2 + x_lo), y: 4, z: 8, core: 2. Of those that a mesh axis runs over, the one named last changes fastest.
Arguments:
- x_ckpt: bfloat16 [4096, 5120], P(('dp', 'tensor')), may hold values from -6 to 6
- d_out: bfloat16 [4096, 5120], P(('dp', 'tensor')), may hold values from -24 to 24
- norm_gain: bfloat16 [5120], replicated, may hold values from 0.099609375 to 1.8984375
- w_query: bfloat16 [5120, 3072], P('dp', 'tensor'), may hold values from -0.078125 to 0.078125
- w_key: bfloat16 [5120, 1024], P('dp', 'tensor'), may hold values from -0.078125 to 0.078125
- w_value: bfloat16 [5120, 1024], P('dp', 'tensor'), may hold values from -0.078125 to 0.078125
- w_out: bfloat16 [3072, 5120], P('tensor', 'dp'), may hold values from -0.109375 to 0.109375
- key_cache: bfloat16 [32, 1024, 1024], P('dp', None, 'tensor')
- value_cache: bfloat16 [32, 1024, 1024], P('dp', None, 'tensor'), may hold values from -6 to 6
- slab_start: int32 [32], P('dp'), may hold values from 0 to 8191
- prefix_len: int32 [32], P('dp'), may hold values from 128 to 1024, as said below
Outputs:
- d_input: bfloat16 [4096, 5120], P(('dp', 'tensor'))
- grad_query: bfloat16 [5120, 3072], P('dp', 'tensor')
- grad_key: bfloat16 [5120, 1024], P('dp', 'tensor')
- grad_value: bfloat16 [5120, 1024], P('dp', 'tensor')
- grad_out: bfloat16 [3072, 5120], P('tensor', 'dp')
- grad_gain: float32 [5120], P(('dp', 'tensor'))
The draws below stay inside these ranges and needn't reach their ends.
Inputs may be any that keep to these rules, and one draw needn't show every extreme that they name: `prefix_len`: one data group has all 1024 slots live in every draw.
All inputs are finite; a program needn't handle non-finite values.
Results may differ from the reference program's by a relative error of at most 0.03.
Values may be sent and summed in bfloat16 or wider, within the bound.
No kernel may reach another device: no remote copies, remote signals or barrier semaphores. Data moves between devices by JAX's collectives and lax.ppermute only.
A program may use at most 128 MiB of HBM per device.

```python
import math
import jax
import jax.numpy as jnp
from jax import lax

D = 5120
KVH = 8
HD = 128
QPER = 3
SLAB = 128
PREFIX = 1024
TOKENS = 4096
QHEADS = 24
N_DP = 32


def draw_key_cache(key, part):
    key = jax.random.fold_in(key, 11)
    entries_key = jax.random.fold_in(key, 0)
    shape = (N_DP, PREFIX, KVH * HD)
    entries = jax.random.normal(entries_key, shape, jnp.float32)
    return entries.astype(jnp.bfloat16)


def draw_prefix_len(key, part):
    key = jax.random.fold_in(key, 23)
    length_key, pick_key = jax.random.split(key)
    lengths = jax.random.randint(length_key, (N_DP,), PREFIX // 8, PREFIX + 1)
    chosen = jax.random.randint(pick_key, (), 0, N_DP)
    return jnp.where(jnp.arange(N_DP) == chosen, PREFIX, lengths).astype(jnp.int32)


def plant(values, rng, low, high):
    longest = values.shape.index(max(values.shape))
    spots = []
    for shift in (0, 1):
        where = [jax.random.randint(jax.random.fold_in(rng, axis), (), 0, length) for axis, length in enumerate(values.shape)]
        where[longest] = (where[longest] + shift) % values.shape[longest]
        spots.append(tuple(where))
    return values.at[spots[0]].set(low).at[spots[1]].set(high)


def raised(values, key, source, target, blocks, factor):
    def block_of(dim):
        return (jnp.arange(values.shape[dim]) // (values.shape[dim] // blocks)).reshape((-1,) + (1,) * (values.ndim - 1 - dim))

    first = jax.random.permutation(key, blocks)[block_of(target)]
    second = (block_of(target) + blocks // 2) % blocks
    return jnp.where((block_of(source) == first) | (block_of(source) == second), factor * values, values)


def levels(own_key, shape, cuts, low, high):
    gain = 1.0
    for position, parts in cuts:
        heights = jax.random.uniform(jax.random.fold_in(jax.random.fold_in(own_key, 6), position), (parts,), jnp.float32, low / len(cuts), high / len(cuts))
        gain = gain * jnp.repeat(jnp.exp(heights), shape[position] // parts).reshape((-1,) + (1,) * (len(shape) - 1 - position))
    return gain


def centred(own_key, shape, scale, bound, cuts=(), kind=jnp.bfloat16):
    gain = levels(own_key, shape, cuts, -0.22, 0.18) if cuts else 1.0
    values = jax.random.normal(own_key, shape, jnp.float32) * scale * gain
    return jnp.minimum(jnp.maximum(values, -bound), bound).astype(kind)


def bell_draw_with(own_key, extent, scale, most, shards, heavy, held_as=jnp.bfloat16):
    array = scale * jax.random.normal(own_key, extent, jnp.float32)
    if shards:
        array = array * levels(own_key, extent, shards, -0.22, 0.18)
    return jnp.clip(raised(array, jax.random.fold_in(own_key, 3), *heavy), -most, most).astype(held_as)


def setup_inputs(seed: int = 0) -> dict:
    key_of = jax.random.split(jax.random.key(seed), 12)
    return {
        "x_ckpt": centred(key_of[0], (TOKENS, D), 1.0, 6.0, ((0, 256),)),
        "d_out": bell_draw_with(key_of[1], (TOKENS, D), 1.0, 24.0, ((0, 256),), (0, 1, 256, 6.0)),
        "norm_gain": jnp.clip(1.0 + 0.18 * jax.random.normal(key_of[2], (D,), jnp.float32), 0.099609375, 1.8984375).astype(jnp.bfloat16),
        "w_query": centred(key_of[3], (D, QHEADS * HD), D ** -0.5, 0.078125, ((0, 32), (1, 8))),
        "w_key": centred(key_of[4], (D, KVH * HD), D ** -0.5, 0.078125, ((0, 32), (1, 8))),
        "w_value": centred(key_of[5], (D, KVH * HD), D ** -0.5, 0.078125, ((0, 32), (1, 8))),
        "w_out": centred(key_of[6], (QHEADS * HD, D), (QHEADS * HD) ** -0.5, 0.109375, ((0, 8), (1, 32))),
        "key_cache": draw_key_cache(jax.random.fold_in(key_of[11], 71), 0),
        "value_cache": centred(key_of[8], (N_DP, PREFIX, KVH * HD), 1.0, 6.0, ((0, 32), (2, 8))),
        "slab_start": plant(jax.random.randint(key_of[9], (N_DP,), 0, 8192), jax.random.fold_in(key_of[9], 1), 0, 8191).astype(jnp.int32),
        "prefix_len": draw_prefix_len(jax.random.fold_in(key_of[11], 71), 0),
    }


EPS = 1e-06
THETA = 1000000.0

def angle_tables(start, count, width):
    positions = (start + jnp.arange(count, dtype=jnp.int32)).astype(jnp.float32)
    freqs = jnp.power(jnp.float32(THETA), jnp.arange(width // 2, dtype=jnp.float32) * (-2.0 / width))
    phase = positions[:, None] * freqs[None, :]
    return (jnp.cos(phase)[:, None, :], jnp.sin(phase)[:, None, :])

def rotate(vectors, cosine, sine):
    half = vectors.shape[-1] // 2
    first = vectors[..., :half]
    second = vectors[..., half:]
    return jnp.concatenate([first * cosine - second * sine, second * cosine + first * sine], axis=-1)

def unrotate(vectors, cosine, sine):
    half = vectors.shape[-1] // 2
    first = vectors[..., :half]
    second = vectors[..., half:]
    return jnp.concatenate([first * cosine + second * sine, second * cosine - first * sine], axis=-1)

def round_low(values):
    return lax.optimization_barrier(values.astype(jnp.bfloat16)).astype(jnp.float32)

def reference(x_ckpt, d_out, norm_gain, w_query, w_key, w_value, w_out, key_cache, value_cache, slab_start, prefix_len):
    norm_weight = norm_gain.astype(jnp.float32)
    heads = QPER * KVH

    def one_group(carry, slab):
        x_rows, output_gradient_rows, k_cache, v_cache, start, limit = slab
        input_float = x_rows.astype(jnp.float32)
        reciprocal_root_mean = lax.rsqrt(lax.optimization_barrier(jnp.mean(input_float * input_float, axis=1, keepdims=True)) + EPS)
        normalized_input = input_float * reciprocal_root_mean
        normalized_rows = (normalized_input * norm_weight).astype(jnp.bfloat16)
        raw_q = jnp.dot(normalized_rows, w_query, preferred_element_type=jnp.float32)
        raw_k = jnp.dot(normalized_rows, w_key, preferred_element_type=jnp.float32)
        raw_v = jnp.dot(normalized_rows, w_value, preferred_element_type=jnp.float32)
        cosine, sine = angle_tables(start, SLAB, HD)
        queries = rotate(raw_q.reshape(SLAB, heads, HD), cosine, sine).astype(jnp.bfloat16)
        keys_new = rotate(raw_k.reshape(SLAB, KVH, HD), cosine, sine).astype(jnp.bfloat16)
        values_new = raw_v.reshape(SLAB, KVH, HD).astype(jnp.bfloat16)
        keys = jnp.concatenate([k_cache.reshape(PREFIX, KVH, HD), keys_new], 0).astype(jnp.float32)
        vals = jnp.concatenate([v_cache.reshape(PREFIX, KVH, HD), values_new], 0).astype(jnp.float32)
        query_groups = queries.reshape(SLAB, KVH, QPER, HD).astype(jnp.float32)
        scores = jnp.einsum('tgqd,jgd->gqtj', query_groups, keys) / math.sqrt(HD)
        slot = jnp.arange(PREFIX + SLAB, dtype=jnp.int32)[None, :]
        token = jnp.arange(SLAB, dtype=jnp.int32)[:, None]
        valid = jnp.where(slot < PREFIX, slot < limit, slot - PREFIX <= token)
        top = lax.optimization_barrier(jnp.max(jnp.where(valid, scores, -jnp.inf), axis=-1, keepdims=True))
        expd = jnp.where(valid, jnp.exp(scores - top), 0.0)
        weights = expd / lax.optimization_barrier(jnp.sum(expd, axis=-1, keepdims=True))
        probs = round_low(weights)
        attended = jnp.einsum('gqtj,jgd->tgqd', probs, vals).reshape(SLAB, heads * HD).astype(jnp.bfloat16)
        d_attended = jnp.dot(output_gradient_rows, w_out.T, preferred_element_type=jnp.float32).astype(jnp.bfloat16)
        out_part = jnp.dot(attended.T, output_gradient_rows, preferred_element_type=jnp.float32)
        attended_f = attended.astype(jnp.float32).reshape(SLAB, KVH, QPER, HD)
        d_attended_f = d_attended.astype(jnp.float32).reshape(SLAB, KVH, QPER, HD)
        delta = lax.optimization_barrier(jnp.sum(d_attended_f * attended_f, axis=-1)).transpose(1, 2, 0)
        d_probs = jnp.einsum('tgqd,jgd->gqtj', d_attended_f, vals)
        d_scores = round_low(weights * (d_probs - delta[..., None]) / math.sqrt(HD))
        dq_rot = jnp.einsum('gqtj,jgd->tgqd', d_scores, keys).reshape(SLAB, heads, HD)
        dk_rot = jnp.einsum('gqtj,tgqd->jgd', d_scores[..., PREFIX:], query_groups)
        dv_new = jnp.einsum('gqtj,tgqd->jgd', probs[..., PREFIX:], d_attended_f)
        dq = unrotate(dq_rot, cosine, sine).astype(jnp.bfloat16).reshape(SLAB, heads * HD)
        dk = unrotate(dk_rot, cosine, sine).astype(jnp.bfloat16).reshape(SLAB, KVH * HD)
        dv = dv_new.astype(jnp.bfloat16).reshape(SLAB, KVH * HD)
        part_q = jnp.dot(normalized_rows.T, dq, preferred_element_type=jnp.float32)
        part_k = jnp.dot(normalized_rows.T, dk, preferred_element_type=jnp.float32)
        part_v = jnp.dot(normalized_rows.T, dv, preferred_element_type=jnp.float32)
        normalized_gradient = jnp.dot(dq, w_query.T, preferred_element_type=jnp.float32)
        normalized_gradient = normalized_gradient + jnp.dot(dk, w_key.T, preferred_element_type=jnp.float32)
        normalized_gradient = normalized_gradient + jnp.dot(dv, w_value.T, preferred_element_type=jnp.float32)
        weighted_rows = normalized_gradient * norm_weight
        row_gradients = (output_gradient_rows.astype(jnp.float32) + reciprocal_root_mean * (weighted_rows - normalized_input * lax.optimization_barrier(jnp.mean(weighted_rows * normalized_input, axis=1, keepdims=True)))).astype(jnp.bfloat16)
        norm_weight_piece = lax.optimization_barrier(jnp.sum(normalized_gradient * normalized_input, axis=0))
        sum_q, sum_k, sum_v, sum_out, sum_gain = carry
        carry = (sum_q + round_low(part_q), sum_k + round_low(part_k), sum_v + round_low(part_v), sum_out + round_low(out_part), sum_gain + norm_weight_piece)
        return (carry, row_gradients)
    start_carry = (jnp.zeros((D, heads * HD), jnp.float32), jnp.zeros((D, KVH * HD), jnp.float32), jnp.zeros((D, KVH * HD), jnp.float32), jnp.zeros((heads * HD, D), jnp.float32), jnp.zeros((D,), jnp.float32))
    slabs = (x_ckpt.reshape(N_DP, SLAB, D), d_out.reshape(N_DP, SLAB, D), key_cache, value_cache, slab_start.astype(jnp.int32), prefix_len.astype(jnp.int32))
    totals, row_gradients = lax.scan(one_group, start_carry, slabs)
    sum_q, sum_k, sum_v, sum_out, sum_gain = totals
    return (row_gradients.reshape(TOKENS, D), sum_q.astype(jnp.bfloat16), sum_k.astype(jnp.bfloat16), sum_v.astype(jnp.bfloat16), sum_out.astype(jnp.bfloat16), sum_gain)
```

```python
import functools
import math

import jax
import jax.numpy as jnp
from jax import lax
from jax.experimental import pallas as pl
from jax.experimental.pallas import tpu as pltpu
from jax.sharding import Mesh
from jax.sharding import PartitionSpec as P

HD = 128
QPER = 3
EPS = 1e-06
THETA = 1000000.0

Z = 8
Q = 4
T = 8
QUARTER = ("xh", "c")
HEADS = ("y", "xl")
PLANE = ("xh", "c", "y", "xl")
VMEM = 48 * 1024 * 1024
F32 = jnp.float32
BF16 = jnp.bfloat16


def call(kernel, outs, n_in, smem=0, scratch=(), flops=0, nbytes=0, trans=0):
    specs = [pl.BlockSpec(memory_space=pltpu.SMEM)] * smem
    specs += [pl.BlockSpec(memory_space=pltpu.VMEM)] * (n_in - smem)
    return pl.pallas_call(
        kernel,
        out_shape=outs,
        in_specs=specs,
        out_specs=jax.tree.map(lambda _: pl.BlockSpec(memory_space=pltpu.VMEM), outs),
        scratch_shapes=list(scratch),
        compiler_params=pltpu.CompilerParams(vmem_limit_bytes=VMEM),
        cost_estimate=pl.CostEstimate(flops=flops, bytes_accessed=nbytes, transcendentals=trans),
    )


def sds(shape, dtype=BF16):
    return jax.ShapeDtypeStruct(shape, dtype)


def dot(a, b, ca, cb):
    return lax.dot_general(a, b, (((ca,), (cb,)), ((), ())), preferred_element_type=F32)


def prep_weights(wq, wk, wv, wo, qkv, wot):
    qkv[:, :384] = wq[...]
    qkv[:, 384:512] = wk[...]
    qkv[:, 512:640] = wv[...]
    wot[...] = wo[...].T


def prep_tokens(z_ref, x, dy, gain, n_out, o_out):
    z = z_ref[0]
    xf = x[...].astype(F32)
    inv = lax.rsqrt(jnp.mean(xf * xf, axis=1, keepdims=True) + EPS)
    for s in range(Z):
        start = pl.multiple_of(lax.rem(z + (Z - s), Z) * 640, 128)
        piece = x[:, pl.ds(start, 640)].astype(F32) * inv
        piece = (piece * gain[:, pl.ds(start, 640)].astype(F32)).astype(BF16)
        grad = dy[:, pl.ds(start, 640)]
        for q in range(Q):
            n = piece[:, 160 * q : 160 * (q + 1)]
            o = grad[:, 160 * q : 160 * (q + 1)]
            for t in range(T):
                n_out[q, t, :, 160 * s : 160 * (s + 1)] = n
                o_out[q, t, :, 160 * s : 160 * (s + 1)] = o


def project(tokens, *refs):
    blocks, out, w = refs[:Z], refs[Z], refs[Z + 1]
    for s in range(Z):
        w[160 * s : 160 * (s + 1), :] = blocks[s][...]
    for r in range(4):
        rows = slice(128 * r, 128 * (r + 1))
        out[r] = dot(tokens[rows, :], w[...], 1, 0).astype(BF16)


def heads_to_rows(a):
    return jnp.concatenate([a[:, HD * h : HD * (h + 1)] for h in range(QPER)], axis=0)


def rows_to_heads(a):
    n = a.shape[0] // QPER
    return jnp.concatenate([a[n * h : n * (h + 1), :] for h in range(QPER)], axis=1)


def attend(limit_ref, parts, cosf, sinf, kc, vc, q_out, k_out, v_out, w_out, att_out):
    raw = parts[0].astype(F32) + parts[1].astype(F32) + parts[2].astype(F32) + parts[3].astype(F32)
    cos, sin = cosf[...], sinf[...]

    def rotate(v):
        return v * cos + jnp.roll(v, HD // 2, axis=1) * sin

    q = jnp.concatenate(
        [rotate(raw[:, HD * h : HD * (h + 1)]) for h in range(QPER)], axis=0
    ).astype(BF16)
    k = rotate(raw[:, 384:512]).astype(BF16)
    v = raw[:, 512:640].astype(BF16)
    q_out[...] = q
    k_out[...] = k
    v_out[...] = v
    rows, slots, new = q.shape[0], kc.shape[0], k.shape[0]
    scale = 1.0 / math.sqrt(HD)
    old_s = dot(q, kc[...], 1, 1) * scale
    new_s = dot(q, k, 1, 1) * scale
    old_ok = lax.broadcasted_iota(jnp.int32, (rows, slots), 1) < limit_ref[0]
    token = lax.rem(lax.broadcasted_iota(jnp.int32, (rows, new), 0), new)
    new_ok = lax.broadcasted_iota(jnp.int32, (rows, new), 1) <= token
    old_s = jnp.where(old_ok, old_s, -jnp.inf)
    new_s = jnp.where(new_ok, new_s, -jnp.inf)
    top = jnp.maximum(
        jnp.max(old_s, axis=1, keepdims=True), jnp.max(new_s, axis=1, keepdims=True)
    )
    old_e = jnp.exp(old_s - top)
    new_e = jnp.exp(new_s - top)
    total = jnp.sum(old_e, axis=1, keepdims=True) + jnp.sum(new_e, axis=1, keepdims=True)
    share = 1.0 / total
    old_w = old_e * share
    new_w = new_e * share
    w_out[:, :slots] = old_w
    w_out[:, slots:] = new_w
    att = dot(old_w.astype(BF16), vc[...], 1, 0) + dot(new_w.astype(BF16), v, 1, 0)
    att_out[...] = rows_to_heads(att.astype(BF16))


def attend_grad(parts, att, w, q, k, v, cosf, sinf, kc, vc, out):
    da = parts[0].astype(F32) + parts[1].astype(F32) + parts[2].astype(F32) + parts[3].astype(F32)
    da = heads_to_rows(da.astype(BF16))
    at = heads_to_rows(att[...])
    delta = jnp.sum(da.astype(F32) * at.astype(F32), axis=1, keepdims=True)
    slots = kc.shape[0]
    scale = 1.0 / math.sqrt(HD)
    old_d = dot(da, vc[...], 1, 1)
    new_d = dot(da, v[...], 1, 1)
    new_w = w[:, slots:]
    old_ds = (w[:, :slots] * (old_d - delta) * scale).astype(BF16)
    new_ds = (new_w * (new_d - delta) * scale).astype(BF16)
    dq = dot(old_ds, kc[...], 1, 0) + dot(new_ds, k[...], 1, 0)
    dk = dot(new_ds, q[...], 0, 0)
    dv = dot(new_w.astype(BF16), da, 0, 0)
    cos, sin = cosf[...], sinf[...]

    def unrotate(a):
        return a * cos - jnp.roll(a, HD // 2, axis=1) * sin

    for h in range(QPER):
        out[:, HD * h : HD * (h + 1)] = unrotate(dq[128 * h : 128 * (h + 1), :]).astype(BF16)
    out[:, 384:512] = unrotate(dk).astype(BF16)
    out[:, 512:640] = dv.astype(BF16)


def weight_grad(tokens, cot, out, c):
    for xh in range(2):
        for core in range(2):
            g = 2 * xh + core
            c[128 * g : 128 * (g + 1), :] = cot[core, xh]
    for s in range(Z):
        part = tokens[:, 160 * s : 160 * (s + 1)]
        out[s] = dot(part, c[...], 0, 0).astype(BF16)


def input_grad(tokens, cot, *refs):
    blocks, out, gain_out, w = refs[:Z], refs[Z], refs[Z + 1], refs[Z + 2]
    for s in range(Z):
        w[160 * s : 160 * (s + 1), :] = blocks[s][...]
    total = jnp.zeros((1, Z * 160), F32)
    for xh in range(2):
        for core in range(2):
            g = 2 * xh + core
            rows = slice(128 * g, 128 * (g + 1))
            dn = dot(cot[core, xh], w[...], 1, 1)
            out[rows, :] = dn.astype(BF16)
            total = total + jnp.sum(dn * tokens[rows, :].astype(F32), axis=0, keepdims=True)
    gain_out[...] = total


def finish(z_ref, parts, x, dy, gain, out, dn):
    z = z_ref[0]
    sums = []
    for q in range(Q):
        a = parts[q, 0].astype(F32)
        for t in range(1, T):
            a = a + parts[q, t].astype(F32)
        sums.append(a)
    for s in range(Z):
        start = pl.multiple_of(lax.rem(z + (Z - s), Z) * 640, 128)
        dn[:, pl.ds(start, 640)] = jnp.concatenate(
            [sums[q][:, 160 * s : 160 * (s + 1)] for q in range(Q)], axis=1
        )
    xf = x[...].astype(F32)
    inv = lax.rsqrt(jnp.mean(xf * xf, axis=1, keepdims=True) + EPS)
    xhat = xf * inv
    scaled = dn[...] * gain[...].astype(F32)
    mean = jnp.mean(scaled * xhat, axis=1, keepdims=True)
    out[...] = (dy[...].astype(F32) + inv * (scaled - xhat * mean)).astype(BF16)


def shift(a, by):
    return lax.ppermute(a, "z", [(i, (i + by) % Z) for i in range(Z)])


def ring_gather(a):
    blocks = [None] * Z
    blocks[0] = ahead = back = a
    for k in range(1, 5):
        ahead = shift(ahead, 1)
        blocks[k] = ahead
        if k < 4:
            back = shift(back, -1)
            blocks[Z - k] = back
    return blocks


def ring_scatter(g):
    def add(a, b):
        return (a.astype(F32) + b.astype(F32)).astype(BF16)

    back, ahead = g[4], g[5]
    for k in range(1, 5):
        back = shift(back, -1)
        if k < 4:
            back = add(back, g[4 - k])
            ahead = shift(ahead, 1)
            if k < 3:
                ahead = add(ahead, g[5 + k])
    return g[0].astype(F32) + back.astype(F32) + ahead.astype(F32)


def body(x, dy, gain, wq, wk, wv, wo, kc, vc, slab_start, prefix_len):
    z = lax.axis_index("z").astype(jnp.int32)
    zs = z.reshape(1)
    gain_row = gain.reshape(1, -1)
    kc, vc = kc.reshape(1024, HD), vc.reshape(1024, HD)

    wqkv, wot = call(
        prep_weights, (sds((160, 640)), sds((160, 384))), 4, nbytes=1 << 20
    )(wq, wk, wv, wo)
    w_blocks = ring_gather(wqkv)
    n_send, o_send = call(
        prep_tokens, (sds((Q, T, 16, 1280)), sds((Q, T, 16, 1280))), 4, smem=1, nbytes=3 << 20
    )(zs, x, dy, gain_row)

    def spread(a):
        return lax.all_to_all(a.reshape(Q * T, 16, 1280), PLANE, 0, 0).reshape(512, 1280)

    n_all = spread(n_send)
    o_all = spread(o_send)
    o_blocks = ring_gather(wot)

    positions = (slab_start[0] + jnp.arange(128, dtype=jnp.int32)).astype(F32)
    freqs = jnp.power(F32(THETA), jnp.arange(HD // 2, dtype=F32) * (-2.0 / HD))
    phase = positions[:, None] * freqs[None, :]
    cos, sin = jnp.cos(phase), jnp.sin(phase)
    cosf = jnp.concatenate([cos, cos], axis=1)
    sinf = jnp.concatenate([-sin, sin], axis=1)

    def projected(tokens, blocks):
        cols = blocks[0].shape[1]
        part = call(
            project,
            sds((Q, 128, cols)),
            1 + Z,
            scratch=[pltpu.VMEM((1280, cols), BF16)],
            flops=2 * 512 * 1280 * cols,
            nbytes=4 << 20,
        )(tokens, *blocks)
        return lax.all_to_all(part, QUARTER, 0, 0)

    qkv_parts = projected(n_all, w_blocks)
    q, k, v, w, att = call(
        attend,
        (sds((384, HD)), sds((128, HD)), sds((128, HD)), sds((384, 1152), F32), sds((128, 384))),
        6,
        smem=1,
        flops=4 * 384 * 1152 * HD,
        nbytes=4 << 20,
        trans=384 * 1152,
    )(prefix_len, qkv_parts, cosf, sinf, kc, vc)

    def gather4(a):
        return lax.all_gather(lax.all_gather(a, "xh"), "c")

    att4 = gather4(att)

    def grads(tokens, cot):
        cols = cot.shape[-1]
        return call(
            weight_grad,
            sds((Z, 160, cols)),
            2,
            scratch=[pltpu.VMEM((512, cols), BF16)],
            flops=2 * 512 * 1280 * cols,
            nbytes=4 << 20,
        )(tokens, cot)

    da_parts = projected(o_all, o_blocks)
    g_out = grads(o_all, att4)
    out_sum = ring_scatter(g_out)
    dqkv = call(
        attend_grad, sds((128, 640)), 10, flops=6 * 384 * 1152 * HD, nbytes=4 << 20
    )(da_parts, att, w, q, k, v, cosf, sinf, kc, vc)
    dqkv4 = gather4(dqkv)
    g_qkv = grads(n_all, dqkv4)
    qkv_sum = ring_scatter(g_qkv)
    dn, gain_part = call(
        input_grad,
        (sds((512, 1280)), sds((1, 1280), F32)),
        2 + Z,
        scratch=[pltpu.VMEM((1280, 640), BF16)],
        flops=2 * 512 * 1280 * 640,
        nbytes=4 << 20,
    )(n_all, dqkv4, *w_blocks)
    dn_parts = lax.all_to_all(dn.reshape(Q * T, 16, 1280), PLANE, 0, 0)
    d_input = call(
        finish, sds((16, 5120)), 5, smem=1, scratch=[pltpu.VMEM((16, 5120), F32)], nbytes=2 << 20
    )(zs, dn_parts.reshape(Q, T, 16, 1280), x, dy, gain_row)

    by_s = gain_part.reshape(Z, T, 20)[::-1]
    by_z = lax.dynamic_slice_in_dim(jnp.concatenate([by_s, by_s], axis=0), Z - 1 - z, Z, axis=0)
    pieces = lax.all_to_all(by_z.reshape(Z * T, 20), ("z",) + HEADS, 0, 0, tiled=True)
    own = (z * Q + lax.axis_index(QUARTER)) * T + lax.axis_index(HEADS)
    own_gain = lax.dynamic_slice_in_dim(gain, own * 20, 20).astype(F32)
    grad_gain = jnp.sum(pieces, axis=0) / own_gain

    grads_qkv = qkv_sum.astype(BF16)
    return (
        d_input,
        grads_qkv[:, :384],
        grads_qkv[:, 384:512],
        grads_qkv[:, 512:640],
        out_sum.astype(BF16).T,
        grad_gain,
    )


def solution(mesh):
    fine = Mesh(mesh.devices.reshape(8, 2, 2, 4, 2), ("z", "xh", "c", "y", "xl"))
    dp = ("z", "xh", "c")
    both = dp + HEADS
    return jax.shard_map(
        body,
        mesh=fine,
        in_specs=(
            P(both, None),
            P(both, None),
            P(),
            P(dp, HEADS),
            P(dp, HEADS),
            P(dp, HEADS),
            P(HEADS, dp),
            P(dp, None, HEADS),
            P(dp, None, HEADS),
            P(dp),
            P(dp),
        ),
        out_specs=(
            P(both, None),
            P(dp, HEADS),
            P(dp, HEADS),
            P(dp, HEADS),
            P(HEADS, dp),
            P(both),
        ),
        check_vma=False,
    )
```

```python
import math

import jax
import jax.numpy as jnp
from jax import lax
from jax.experimental import pallas as pl
from jax.experimental.pallas import tpu as pltpu
from jax.sharding import Mesh
from jax.sharding import PartitionSpec as P

HD = 128
QPER = 3
EPS = 1e-06
THETA = 1000000.0

Z = 8
Q = 4
T = 8
QUARTER = ("xh", "c")
HEADS = ("y", "xl")
PLANE = ("xh", "c", "y", "xl")
VMEM = 16 * 1024 * 1024
ALL = 60 * 1024 * 1024
F32 = jnp.float32
BF16 = jnp.bfloat16


def call(
    kernel, outs, shapes, smem=0, far=0, far_out=0, scratch=(), flops=0, nbytes=0, trans=0, grant=VMEM
):
    near = len(shapes) - smem - far
    return pl.pallas_call(
        kernel,
        out_shape=tuple(outs),
        in_specs=[pl.BlockSpec(memory_space=pltpu.SMEM)] * smem
        + [pl.BlockSpec()] * near
        + [pl.BlockSpec(memory_space=pltpu.HBM)] * far,
        out_specs=tuple([pl.BlockSpec()] * (len(outs) - far_out))
        + tuple([pl.BlockSpec(memory_space=pltpu.HBM)] * far_out),
        scratch_shapes=list(scratch),
        compiler_params=pltpu.CompilerParams(vmem_limit_bytes=grant),
        cost_estimate=pl.CostEstimate(flops=flops, bytes_accessed=nbytes, transcendentals=trans),
    )


def sds(shape, dtype=BF16):
    return jax.ShapeDtypeStruct(shape, dtype)


def run(kernel, outs, args, **kw):
    return call(kernel, outs, [sds(a.shape, a.dtype) for a in args], **kw)(*args)


def dot(a, b, ca, cb):
    return lax.dot_general(a, b, (((ca,), (cb,)), ((), ())), preferred_element_type=F32)


def copies_of(pairs, sems):
    made = [pltpu.make_async_copy(src, dst, sems.at[i]) for i, (src, dst) in enumerate(pairs)]
    for copy in made:
        copy.start()
    return made


def join(wq, wk, wv, wo, out):
    out[:, :384] = wq[...]
    out[:, 384:512] = wk[...]
    out[:, 512:640] = wv[...]
    out[:, 640:] = wo[...]


def split(total, q_out, k_out, v_out, o_out):
    q_out[...] = total[:, :384]
    k_out[...] = total[:, 384:512]
    v_out[...] = total[:, 512:640]
    o_out[...] = total[:, 640:]


def prep_tokens(gain, x_far, dy_far, out_far, x, dy, out, sems):
    copy_x, copy_dy = copies_of([(x_far, x), (dy_far, dy)], sems)
    copy_x.wait()
    xf = x[...].astype(F32)
    inv = lax.rsqrt(jnp.mean(xf * xf, axis=1, keepdims=True) + EPS)
    n = (xf * inv * gain[...].reshape(1, -1).astype(F32)).astype(BF16)
    copy_dy.wait()
    sent = []
    for q in range(Q):
        cols = [slice((Q * z + q) * 160, (Q * z + q + 1) * 160) for z in range(Z)]
        row = jnp.concatenate([n[:, c] for c in cols] + [dy[:, c] for c in cols], axis=1)
        for t in range(T):
            out[q * T + t] = row
        part = pl.ds(q * T, T)
        copy = pltpu.make_async_copy(out.at[part], out_far.at[part], sems.at[2 + q])
        copy.start()
        sent.append(copy)
    for copy in sent:
        copy.wait()


def project(g_ref, tokens, w, keep, send, held):
    for first, last, at in ((0, 384, 0), (384, 640, 0), (640, 1024, 1280)):
        part = dot(tokens[:, at : at + 1280], w[:, first:last], 1, 0).astype(BF16)
        for g in range(Q):
            held[g_ref[0] ^ g, :, first:last] = part[128 * g : 128 * (g + 1), :]
    for xh in range(2):
        keep[xh] = held[2 * xh]
        send[xh] = held[2 * xh + 1]


def add(keep, pair, out):
    out[...] = (keep[1].astype(F32) + pair[1].astype(F32)).astype(BF16)


def heads_to_rows(a):
    return jnp.concatenate([a[:, HD * h : HD * (h + 1)] for h in range(QPER)], axis=0)


def rows_to_heads(a):
    n = a.shape[0] // QPER
    return jnp.concatenate([a[n * h : n * (h + 1), :] for h in range(QPER)], axis=1)


def attend(limit_ref, mine, pair, far, cosf, sinf, kc, vc, out):
    raw = mine[0].astype(F32) + pair[0].astype(F32) + far[...].astype(F32)
    cos, sin = cosf[...], sinf[...]

    def rotate(v):
        return v * cos + jnp.roll(v, HD // 2, axis=1) * sin

    def unrotate(v):
        return v * cos - jnp.roll(v, HD // 2, axis=1) * sin

    q = jnp.concatenate(
        [rotate(raw[:, HD * h : HD * (h + 1)]) for h in range(QPER)], axis=0
    ).astype(BF16)
    k = rotate(raw[:, 384:512]).astype(BF16)
    v = raw[:, 512:640].astype(BF16)
    da = heads_to_rows(raw[:, 640:].astype(BF16))
    rows, slots, new = q.shape[0], kc.shape[0], k.shape[0]
    scale = 1.0 / math.sqrt(HD)
    old_s = dot(q, kc[...], 1, 1) * scale
    new_s = dot(q, k, 1, 1) * scale
    old_ok = lax.broadcasted_iota(jnp.int32, (rows, slots), 1) < limit_ref[0]
    token = lax.rem(lax.broadcasted_iota(jnp.int32, (rows, new), 0), new)
    new_ok = lax.broadcasted_iota(jnp.int32, (rows, new), 1) <= token
    old_s = jnp.where(old_ok, old_s, -jnp.inf)
    new_s = jnp.where(new_ok, new_s, -jnp.inf)
    top = jnp.maximum(
        jnp.max(old_s, axis=1, keepdims=True), jnp.max(new_s, axis=1, keepdims=True)
    )
    old_e = jnp.exp(old_s - top)
    new_e = jnp.exp(new_s - top)
    total = jnp.sum(old_e, axis=1, keepdims=True) + jnp.sum(new_e, axis=1, keepdims=True)
    share = 1.0 / total
    old_w = old_e * share
    new_w = new_e * share
    new_p = new_w.astype(BF16)
    att = (dot(old_w.astype(BF16), vc[...], 1, 0) + dot(new_p, v, 1, 0)).astype(BF16)
    out[:, 640:] = rows_to_heads(att)

    delta = jnp.sum(da.astype(F32) * att.astype(F32), axis=1, keepdims=True)
    old_ds = (old_w * (dot(da, vc[...], 1, 1) - delta) * scale).astype(BF16)
    new_ds = (new_w * (dot(da, v, 1, 1) - delta) * scale).astype(BF16)
    dq = dot(old_ds, kc[...], 1, 0) + dot(new_ds, k, 1, 0)
    dk = dot(new_ds, q, 0, 0)
    dv = dot(new_p, da, 0, 0)
    for h in range(QPER):
        out[:, HD * h : HD * (h + 1)] = unrotate(dq[128 * h : 128 * (h + 1), :]).astype(BF16)
    out[:, 384:512] = unrotate(dk).astype(BF16)
    out[:, 512:640] = dv.astype(BF16)


def gather_rows(g_ref, cots, cot):
    for d, block in enumerate(cots):
        rows = pl.ds(pl.multiple_of((g_ref[0] ^ d) * 128, 128), 128)
        cot[rows, :] = block[:, : cot.shape[1]]


def weight_grad(g_ref, tokens, c0, c1, c2, c3, out, cot):
    gather_rows(g_ref, (c0, c1, c2, c3), cot)
    for r in range(5):
        cols = slice(256 * r, 256 * (r + 1))
        late = slice(1280 + 256 * r, 1280 + 256 * (r + 1))
        out[cols, :640] = dot(tokens[:, cols], cot[:, :640], 0, 0).astype(BF16)
        out[cols, 640:] = dot(tokens[:, late], cot[:, 640:], 0, 0).astype(BF16)


def input_grad(g_ref, tokens, c0, c1, c2, c3, w, out, cot):
    gather_rows(g_ref, (c0, c1, c2, c3), cot)
    sums = []
    for r in range(5):
        cols = slice(256 * r, 256 * (r + 1))
        dn = dot(cot[...], w[cols, :640], 1, 1)
        sums.append(jnp.sum(dn * tokens[:, cols].astype(F32), axis=0, keepdims=True))
        dn = dn.astype(BF16)
        for b in range(Q * T):
            out[b, :, cols] = dn[16 * b : 16 * (b + 1), :]
    total = jnp.concatenate(sums, axis=1)
    total = jnp.concatenate([total[:, 160 * z : 160 * (z + 1)] for z in range(Z)], axis=0)
    high = total.astype(BF16)
    low = (total - high.astype(F32)).astype(BF16)
    both = jnp.concatenate([high, low], axis=0)
    zero = jnp.zeros((16, 108), BF16)
    for t in range(T):
        tile = jnp.concatenate([both[:, 20 * t : 20 * (t + 1)], zero], axis=1)
        for q in range(Q):
            out[q * T + t, :, 1280:] = tile


def finish(g_ref, parts, x, dy, gain, out, gain_out):
    sums = []
    for q in range(Q):
        a = parts[q, 0, :, :1280].astype(F32)
        for t in range(1, T):
            a = a + parts[q, t, :, :1280].astype(F32)
        sums.append(a)
    tile = parts[g_ref[0], 0, :, 1280:].astype(F32)
    for t in range(1, T):
        tile = tile + parts[g_ref[0], t, :, 1280:].astype(F32)
    gain_out[...] = tile[:8, :] + tile[8:, :]
    dn = jnp.concatenate(
        [sums[q][:, 160 * z : 160 * (z + 1)] for z in range(Z) for q in range(Q)], axis=1
    )
    xf = x[...].astype(F32)
    inv = lax.rsqrt(jnp.mean(xf * xf, axis=1, keepdims=True) + EPS)
    xhat = xf * inv
    scaled = dn * gain[...].reshape(1, -1).astype(F32)
    mean = jnp.mean(scaled * xhat, axis=1, keepdims=True)
    out[...] = (dy[...].astype(F32) + inv * (scaled - xhat * mean)).astype(BF16)


def tie(*arrays):
    return lax.optimization_barrier(arrays)


def swap(a, axis):
    return lax.ppermute(a, axis, [(0, 1), (1, 0)])


def body(x, dy, gain, wq, wk, wv, wo, kc, vc, slab_start, prefix_len):
    z = lax.axis_index("z").astype(jnp.int32)
    gs = lax.axis_index(QUARTER).astype(jnp.int32).reshape(1)
    kc, vc = kc.reshape(1024, HD), vc.reshape(1024, HD)

    (w_own,) = run(
        join,
        [sds((160, 1024))],
        (wq, wk, wv, wo.T),
        grant=ALL,
        nbytes=1 << 20,
    )
    x_in, w_own = tie(x, w_own)
    w = lax.all_gather(w_own, "z", axis=0, tiled=True)
    (sent,) = run(
        prep_tokens,
        [sds((Q * T, 16, 2560))],
        (gain, x_in, dy),
        far=2,
        far_out=1,
        scratch=[
            pltpu.VMEM((16, 5120), BF16),
            pltpu.VMEM((16, 5120), BF16),
            pltpu.VMEM((Q * T, 16, 2560), BF16),
            pltpu.SemaphoreType.DMA((2 + Q,)),
        ],
        grant=ALL,
        nbytes=3 << 20,
    )
    tokens = lax.all_to_all(sent, PLANE, 0, 0).reshape(512, 2560)

    positions = (slab_start[0] + jnp.arange(128, dtype=jnp.int32)).astype(F32)
    freqs = jnp.power(F32(THETA), jnp.arange(HD // 2, dtype=F32) * (-2.0 / HD))
    phase = positions[:, None] * freqs[None, :]
    cos, sin = jnp.cos(phase), jnp.sin(phase)
    cosf = jnp.concatenate([cos, cos], axis=1)
    sinf = jnp.concatenate([-sin, sin], axis=1)
    tokens, cosf, sinf = tie(tokens, cosf, sinf)

    keep, send = run(
        project,
        [sds((2, 128, 1024)), sds((2, 128, 1024))],
        (gs, tokens, w),
        smem=1,
        scratch=[pltpu.VMEM((Q, 128, 1024), BF16)],
        flops=2 * 512 * 1280 * 1024,
        nbytes=7 << 20,
    )
    pair = swap(send, "c")
    (passed,) = run(add, [sds((128, 1024))], (keep, pair), nbytes=1 << 20)
    far = swap(passed, "xh")
    (cot,) = run(
        attend,
        [sds((128, 1024))],
        (prefix_len, keep, pair, far, cosf, sinf, kc, vc),
        smem=1,
        flops=10 * 384 * 1152 * HD,
        nbytes=4 << 20,
        trans=384 * 1152,
    )
    across = swap(cot, "xh")
    cots = (cot, swap(cot, "c"), across, swap(across, "c"))
    (grads,) = run(
        weight_grad,
        [sds((1280, 1024))],
        (gs, tokens, *cots),
        smem=1,
        scratch=[pltpu.VMEM((512, 1024), BF16)],
        flops=2 * 512 * 1280 * 1024,
        nbytes=8 << 20,
    )
    late, grads = tie(tokens, grads)
    total = lax.psum_scatter(grads, "z", scatter_dimension=0, tiled=True)
    (dn,) = run(
        input_grad,
        [sds((Q * T, 16, 1408))],
        (gs, late, *cots, w),
        smem=1,
        scratch=[pltpu.VMEM((512, 640), BF16)],
        flops=2 * 512 * 1280 * 640,
        nbytes=7 << 20,
    )
    dn_parts = lax.all_to_all(dn, PLANE, 0, 0)
    d_input, gain_z = run(
        finish,
        [sds((16, 5120)), sds((8, 128), F32)],
        (gs, dn_parts.reshape(Q, T, 16, 1408), x, dy, gain),
        smem=1,
        nbytes=2 << 20,
    )
    pieces = lax.all_to_all(gain_z.reshape(Z, 1, 128), "z", 0, 0)
    own = (z * Q + lax.axis_index(QUARTER)) * T + lax.axis_index(HEADS)
    own_gain = lax.dynamic_slice_in_dim(gain, own * 20, 20).astype(F32)
    grad_gain = jnp.sum(pieces, axis=(0, 1))[:20] / own_gain

    gq, gk, gv, go = run(
        split,
        [sds((160, 384)), sds((160, 128)), sds((160, 128)), sds((160, 384))],
        (total,),
        grant=ALL,
        nbytes=2 << 20,
    )
    return d_input, gq, gk, gv, go.T, grad_gain


def solution(mesh):
    fine = Mesh(mesh.devices.reshape(8, 2, 2, 4, 2), ("z", "xh", "c", "y", "xl"))
    dp = ("z", "xh", "c")
    both = dp + HEADS
    return jax.shard_map(
        body,
        mesh=fine,
        in_specs=(
            P(both, None),
            P(both, None),
            P(),
            P(dp, HEADS),
            P(dp, HEADS),
            P(dp, HEADS),
            P(HEADS, dp),
            P(dp, None, HEADS),
            P(dp, None, HEADS),
            P(dp),
            P(dp),
        ),
        out_specs=(
            P(both, None),
            P(dp, HEADS),
            P(dp, HEADS),
            P(dp, HEADS),
            P(HEADS, dp),
            P(both),
        ),
        check_vma=False,
    )
```

```python
import math

import jax
import jax.numpy as jnp
from jax import lax
from jax.experimental import pallas as pl
from jax.experimental.pallas import tpu as pltpu
from jax.sharding import Mesh
from jax.sharding import PartitionSpec as P

HD = 128
QPER = 3
EPS = 1e-06
THETA = 1000000.0

Z = 8
Q = 4
T = 8
QUARTER = ("xh", "c")
HEADS = ("y", "xl")
PLANE = ("xh", "c", "y", "xl")
VMEM = 16 * 1024 * 1024
ALL = 60 * 1024 * 1024
LONG = 1 << 35
F32 = jnp.float32
BF16 = jnp.bfloat16


def call(
    kernel, outs, shapes, smem=0, far=0, far_out=0, scratch=(), flops=0, nbytes=0, trans=0, grant=VMEM
):
    near = len(shapes) - smem - far
    return pl.pallas_call(
        kernel,
        out_shape=tuple(outs[: len(outs) - far_out])
        + tuple(pltpu.HBM(o.shape, o.dtype) for o in outs[len(outs) - far_out :]),
        in_specs=[pl.BlockSpec(memory_space=pltpu.SMEM)] * smem
        + [pl.BlockSpec()] * near
        + [pl.BlockSpec(memory_space=pltpu.HBM)] * far,
        out_specs=tuple([pl.BlockSpec()] * (len(outs) - far_out))
        + tuple([pl.BlockSpec(memory_space=pltpu.HBM)] * far_out),
        scratch_shapes=list(scratch),
        compiler_params=pltpu.CompilerParams(vmem_limit_bytes=grant),
        cost_estimate=pl.CostEstimate(flops=flops, bytes_accessed=nbytes, transcendentals=trans),
    )


def sds(shape, dtype=BF16):
    return jax.ShapeDtypeStruct(shape, dtype)


def run(kernel, outs, args, far=0, **kw):
    shapes = [sds(a.shape, a.dtype) for a in args]
    near = len(args) - far
    args = list(args[:near]) + [
        pltpu.with_memory_space_constraint(a, pltpu.HBM) for a in args[near:]
    ]
    return call(kernel, outs, shapes, far=far, **kw)(*args)


def dot(a, b, ca, cb):
    return lax.dot_general(a, b, (((ca,), (cb,)), ((), ())), preferred_element_type=F32)


def copies_of(pairs, sems):
    made = [pltpu.make_async_copy(src, dst, sems.at[i]) for i, (src, dst) in enumerate(pairs)]
    for copy in made:
        copy.start()
    return made


def join(wq, wk, wv, wo, out_far, out, sems):
    parts = ((wq, 0, 384), (wk, 384, 512), (wv, 512, 640), (wo, 640, 1024))
    for copy in copies_of([(src, out.at[:, a:b]) for src, a, b in parts], sems):
        copy.wait()
    copy = pltpu.make_async_copy(out, out_far, sems.at[4])
    copy.start()
    copy.wait()


def split(total, q_out, k_out, v_out, o_out):
    q_out[...] = total[:, :384]
    k_out[...] = total[:, 384:512]
    v_out[...] = total[:, 512:640]
    o_out[...] = total[:, 640:]


def prep_tokens(gain, x_far, dy_far, out_far, x, dy, out, sems):
    copy_x, copy_dy = copies_of([(x_far, x), (dy_far, dy)], sems)
    copy_x.wait()
    xf = x[...].astype(F32)
    inv = lax.rsqrt(jnp.mean(xf * xf, axis=1, keepdims=True) + EPS)
    n = (xf * inv * gain[...].reshape(1, -1).astype(F32)).astype(BF16)
    copy_dy.wait()
    sent = []
    for q in range(Q):
        cols = [slice((Q * z + q) * 160, (Q * z + q + 1) * 160) for z in range(Z)]
        row = jnp.concatenate([n[:, c] for c in cols] + [dy[:, c] for c in cols], axis=1)
        for t in range(T):
            out[q * T + t] = row
        part = pl.ds(q * T, T)
        copy = pltpu.make_async_copy(out.at[part], out_far.at[part], sems.at[2 + q])
        copy.start()
        sent.append(copy)
    for copy in sent:
        copy.wait()


def project(g_ref, tokens, w_far, keep, send, w, total, sems):
    halves = (slice(0, 640), slice(640, 1280))
    parts = ((0, 384, 0), (384, 640, 0), (640, 1024, 1280))
    copies = copies_of([(w_far.at[rows], w.at[rows]) for rows in halves], sems)
    copies[0].wait()
    for first, last, at in parts:
        total[:, first:last] = dot(tokens[:, at : at + 640], w[halves[0], first:last], 1, 0)
    copies[1].wait()
    for first, last, at in parts:
        part = dot(tokens[:, at + 640 : at + 1280], w[halves[1], first:last], 1, 0)
        total[:, first:last] += part
    for xh in range(2):
        for core, out in ((0, keep), (1, send)):
            rows = pl.ds(pl.multiple_of((g_ref[0] ^ (2 * xh + core)) * 128, 128), 128)
            out[xh] = total[rows, :].astype(BF16)


def add(keep, pair, out):
    out[...] = (keep[1].astype(F32) + pair[1].astype(F32)).astype(BF16)


def heads_to_rows(a):
    return jnp.concatenate([a[:, HD * h : HD * (h + 1)] for h in range(QPER)], axis=0)


def rows_to_heads(a):
    n = a.shape[0] // QPER
    return jnp.concatenate([a[n * h : n * (h + 1), :] for h in range(QPER)], axis=1)


def attend(limit_ref, mine, pair, far, cosf, sinf, kc, vc, out):
    raw = mine[0].astype(F32) + pair[0].astype(F32) + far[...].astype(F32)
    cos, sin = cosf[...], sinf[...]

    def rotate(v):
        return v * cos + jnp.roll(v, HD // 2, axis=1) * sin

    def unrotate(v):
        return v * cos - jnp.roll(v, HD // 2, axis=1) * sin

    q = jnp.concatenate(
        [rotate(raw[:, HD * h : HD * (h + 1)]) for h in range(QPER)], axis=0
    ).astype(BF16)
    k = rotate(raw[:, 384:512]).astype(BF16)
    v = raw[:, 512:640].astype(BF16)
    da = heads_to_rows(raw[:, 640:].astype(BF16))
    rows, slots, new = q.shape[0], kc.shape[0], k.shape[0]
    scale = 1.0 / math.sqrt(HD)
    old_s = dot(q, kc[...], 1, 1) * scale
    new_s = dot(q, k, 1, 1) * scale
    old_ok = lax.broadcasted_iota(jnp.int32, (rows, slots), 1) < limit_ref[0]
    token = lax.rem(lax.broadcasted_iota(jnp.int32, (rows, new), 0), new)
    new_ok = lax.broadcasted_iota(jnp.int32, (rows, new), 1) <= token
    old_s = jnp.where(old_ok, old_s, -jnp.inf)
    new_s = jnp.where(new_ok, new_s, -jnp.inf)
    top = jnp.maximum(
        jnp.max(old_s, axis=1, keepdims=True), jnp.max(new_s, axis=1, keepdims=True)
    )
    old_e = jnp.exp(old_s - top)
    new_e = jnp.exp(new_s - top)
    total = jnp.sum(old_e, axis=1, keepdims=True) + jnp.sum(new_e, axis=1, keepdims=True)
    share = 1.0 / total
    old_w = old_e * share
    new_w = new_e * share
    new_p = new_w.astype(BF16)
    att = (dot(old_w.astype(BF16), vc[...], 1, 0) + dot(new_p, v, 1, 0)).astype(BF16)
    out[:, 640:] = rows_to_heads(att)

    delta = jnp.sum(da.astype(F32) * att.astype(F32), axis=1, keepdims=True)
    old_ds = (old_w * (dot(da, vc[...], 1, 1) - delta) * scale).astype(BF16)
    new_ds = (new_w * (dot(da, v, 1, 1) - delta) * scale).astype(BF16)
    dq = dot(old_ds, kc[...], 1, 0) + dot(new_ds, k, 1, 0)
    dk = dot(new_ds, q, 0, 0)
    dv = dot(new_p, da, 0, 0)
    for h in range(QPER):
        out[:, HD * h : HD * (h + 1)] = unrotate(dq[128 * h : 128 * (h + 1), :]).astype(BF16)
    out[:, 384:512] = unrotate(dk).astype(BF16)
    out[:, 512:640] = dv.astype(BF16)


def gather_rows(g_ref, cots, cot):
    for d, block in enumerate(cots):
        rows = pl.ds(pl.multiple_of((g_ref[0] ^ d) * 128, 128), 128)
        cot[rows, :] = block[:, : cot.shape[1]]


def weight_grad(g_ref, tokens, c0, c1, c2, c3, cot_out, grad_far, grad, cot, sems):
    gather_rows(g_ref, (c0, c1, c2, c3), cot)
    cot_out[...] = cot[:, :640]
    sent = []
    for r in range(5):
        cols = slice(256 * r, 256 * (r + 1))
        late = slice(1280 + 256 * r, 1280 + 256 * (r + 1))
        grad[cols, :640] = dot(tokens[:, cols], cot[:, :640], 0, 0).astype(BF16)
        grad[cols, 640:] = dot(tokens[:, late], cot[:, 640:], 0, 0).astype(BF16)
        copy = pltpu.make_async_copy(grad.at[cols], grad_far.at[cols], sems.at[r])
        copy.start()
        sent.append(copy)
    for copy in sent:
        copy.wait()


def input_grad(tokens, cot, w_far, out_far, w, out, sems):
    sent = []
    copy_w, copy_w2 = copies_of(
        [(w_far.at[:256, :640], w.at[:256]), (w_far.at[256:, :640], w.at[256:])], sems
    )
    copy_w.wait()
    sums = []
    for r in range(5):
        cols = slice(256 * r, 256 * (r + 1))
        if r == 1:
            copy_w2.wait()
        dn = dot(cot[...], w[cols, :], 1, 1)
        sums.append(jnp.sum(dn * tokens[:, cols].astype(F32), axis=0, keepdims=True))
        dn = dn.astype(BF16)
        for b in range(Q * T):
            out[b, :, cols] = dn[16 * b : 16 * (b + 1), :]
        copy = pltpu.make_async_copy(out.at[:, :, cols], out_far.at[:, :, cols], sems.at[6 + r])
        copy.start()
        sent.append(copy)
    total = jnp.concatenate(sums, axis=1)
    total = jnp.concatenate([total[:, 160 * z : 160 * (z + 1)] for z in range(Z)], axis=0)
    high = total.astype(BF16)
    low = (total - high.astype(F32)).astype(BF16)
    both = jnp.concatenate([high, low], axis=0)
    zero = jnp.zeros((16, 108), BF16)
    for t in range(T):
        tile = jnp.concatenate([both[:, 20 * t : 20 * (t + 1)], zero], axis=1)
        for q in range(Q):
            out[q * T + t, :, 1280:] = tile
    last = pltpu.make_async_copy(out.at[:, :, 1280:], out_far.at[:, :, 1280:], sems.at[11])
    last.start()
    for copy in sent + [last]:
        copy.wait()


def normalize(x, xhat, inv):
    xf = x[...].astype(F32)
    scale = lax.rsqrt(jnp.mean(xf * xf, axis=1, keepdims=True) + EPS)
    xhat[...] = xf * scale
    inv[...] = jnp.broadcast_to(scale, (16, 128))


def gain_sum(g_ref, parts, gain_out):
    tile = parts[g_ref[0], 0, :, 1280:].astype(F32)
    for t in range(1, T):
        tile = tile + parts[g_ref[0], t, :, 1280:].astype(F32)
    gain_out[...] = tile[:8, :] + tile[8:, :]


def finish(parts, xhat, inv, dy, gain, out):
    sums = []
    for q in range(Q):
        a = parts[q, 0, :, :1280].astype(F32)
        for t in range(1, T):
            a = a + parts[q, t, :, :1280].astype(F32)
        sums.append(a)
    dn = jnp.concatenate(
        [sums[q][:, 160 * z : 160 * (z + 1)] for z in range(Z) for q in range(Q)], axis=1
    )
    scaled = dn * gain[...].reshape(1, -1).astype(F32)
    mean = jnp.mean(scaled * xhat[...], axis=1, keepdims=True)
    out[...] = (dy[...].astype(F32) + inv[:, :1] * (scaled - xhat[...] * mean)).astype(BF16)


def tie(*arrays):
    return lax.optimization_barrier(arrays)


def swap(a, axis):
    return lax.ppermute(a, axis, [(0, 1), (1, 0)])


def body(x, dy, gain, wq, wk, wv, wo, kc, vc, slab_start, prefix_len):
    z = lax.axis_index("z").astype(jnp.int32)
    gs = lax.axis_index(QUARTER).astype(jnp.int32).reshape(1)
    kc, vc = kc.reshape(1024, HD), vc.reshape(1024, HD)

    (w_own,) = run(
        join,
        [sds((160, 1024))],
        (wq, wk, wv, wo.T),
        far=4,
        far_out=1,
        scratch=[pltpu.VMEM((160, 1024), BF16), pltpu.SemaphoreType.DMA((5,))],
        nbytes=1 << 20,
    )
    x_in, w_own = tie(x, w_own)
    w = lax.all_gather(w_own, "z", axis=0, tiled=True)
    (sent,) = run(
        prep_tokens,
        [sds((Q * T, 16, 2560))],
        (gain, x_in, dy),
        far=2,
        far_out=1,
        scratch=[
            pltpu.VMEM((16, 5120), BF16),
            pltpu.VMEM((16, 5120), BF16),
            pltpu.VMEM((Q * T, 16, 2560), BF16),
            pltpu.SemaphoreType.DMA((2 + Q,)),
        ],
        grant=ALL,
        nbytes=3 << 20,
    )
    tokens = lax.all_to_all(sent, PLANE, 0, 0).reshape(512, 2560)

    positions = (slab_start[0] + jnp.arange(128, dtype=jnp.int32)).astype(F32)
    freqs = jnp.power(F32(THETA), jnp.arange(HD // 2, dtype=F32) * (-2.0 / HD))
    phase = positions[:, None] * freqs[None, :]
    cos, sin = jnp.cos(phase), jnp.sin(phase)
    cosf = jnp.concatenate([cos, cos], axis=1)
    sinf = jnp.concatenate([-sin, sin], axis=1)
    tokens, cosf, sinf = tie(tokens, cosf, sinf)

    keep, send = run(
        project,
        [sds((2, 128, 1024)), sds((2, 128, 1024))],
        (gs, tokens, w),
        smem=1,
        far=1,
        scratch=[
            pltpu.VMEM((1280, 1024), BF16),
            pltpu.VMEM((512, 1024), F32),
            pltpu.SemaphoreType.DMA((2,)),
        ],
        flops=2 * 512 * 1280 * 1024,
        nbytes=7 << 20,
    )
    pair = swap(send, "c")
    (passed,) = run(add, [sds((128, 1024))], (keep, pair), nbytes=1 << 20)
    far = swap(passed, "xh")
    (cot,) = run(
        attend,
        [sds((128, 1024))],
        (prefix_len, keep, pair, far, cosf, sinf, kc, vc),
        smem=1,
        flops=10 * 384 * 1152 * HD,
        nbytes=4 << 20,
        trans=384 * 1152,
    )
    across = swap(cot, "xh")
    cots = (cot, swap(cot, "c"), across, swap(across, "c"))
    cot4, grads = run(
        weight_grad,
        [sds((512, 640)), sds((1280, 1024))],
        (gs, tokens, *cots),
        smem=1,
        far_out=1,
        scratch=[
            pltpu.VMEM((1280, 1024), BF16),
            pltpu.VMEM((512, 1024), BF16),
            pltpu.SemaphoreType.DMA((5,)),
        ],
        flops=2 * 512 * 1280 * 1024,
        nbytes=8 << 20,
    )
    total = lax.psum_scatter(grads, "z", scatter_dimension=0, tiled=True)
    (dn,) = run(
        input_grad,
        [sds((Q * T, 16, 1408))],
        (tokens, cot4, w),
        far=1,
        far_out=1,
        scratch=[
            pltpu.VMEM((1280, 640), BF16),
            pltpu.VMEM((Q * T, 16, 1408), BF16),
            pltpu.SemaphoreType.DMA((12,)),
        ],
        flops=2 * 512 * 1280 * 640,
        nbytes=7 << 20,
    )
    x_late, dn = tie(x, dn)
    dn_parts = lax.all_to_all(dn, PLANE, 0, 0)
    xhat, inv = run(normalize, [sds((16, 5120), F32), sds((16, 128), F32)], (x_late,), flops=LONG)
    dn_parts = dn_parts.reshape(Q, T, 16, 1408)
    (gain_z,) = run(gain_sum, [sds((8, 128), F32)], (gs, dn_parts), smem=1)
    (d_input,) = run(
        finish,
        [sds((16, 5120))],
        (dn_parts, xhat, inv, dy, gain),
        nbytes=2 << 20,
    )
    pieces = lax.all_to_all(gain_z.reshape(Z, 1, 128), "z", 0, 0)
    own = (z * Q + lax.axis_index(QUARTER)) * T + lax.axis_index(HEADS)
    own_gain = lax.dynamic_slice_in_dim(gain, own * 20, 20).astype(F32)
    grad_gain = jnp.sum(pieces, axis=(0, 1))[:20] / own_gain

    gq, gk, gv, go = run(
        split,
        [sds((160, 384)), sds((160, 128)), sds((160, 128)), sds((160, 384))],
        (total,),
        grant=ALL,
        nbytes=2 << 20,
    )
    return d_input, gq, gk, gv, go.T, grad_gain


def solution(mesh):
    fine = Mesh(mesh.devices.reshape(8, 2, 2, 4, 2), ("z", "xh", "c", "y", "xl"))
    dp = ("z", "xh", "c")
    both = dp + HEADS
    return jax.shard_map(
        body,
        mesh=fine,
        in_specs=(
            P(both, None),
            P(both, None),
            P(),
            P(dp, HEADS),
            P(dp, HEADS),
            P(dp, HEADS),
            P(HEADS, dp),
            P(dp, None, HEADS),
            P(dp, None, HEADS),
            P(dp),
            P(dp),
        ),
        out_specs=(
            P(both, None),
            P(dp, HEADS),
            P(dp, HEADS),
            P(dp, HEADS),
            P(HEADS, dp),
            P(both),
        ),
        check_vma=False,
    )
```

```python
import math

import jax
import jax.numpy as jnp
from jax import lax
from jax.experimental import pallas as pl
from jax.experimental.pallas import tpu as pltpu
from jax.sharding import Mesh
from jax.sharding import PartitionSpec as P

HD = 128
QPER = 3
EPS = 1e-06
THETA = 1000000.0

Z = 8
Q = 4
T = 8
QUARTER = ("xh", "c")
HEADS = ("y", "xl")
PLANE = ("xh", "c", "y", "xl")
VMEM = 16 * 1024 * 1024
LONG = 1 << 35
F32 = jnp.float32
BF16 = jnp.bfloat16


def call(
    kernel, outs, shapes, smem=0, far=0, far_out=0, scratch=(), flops=0, nbytes=0, trans=0, grant=VMEM
):
    near = len(shapes) - smem - far
    return pl.pallas_call(
        kernel,
        out_shape=tuple(outs[: len(outs) - far_out])
        + tuple(pltpu.HBM(o.shape, o.dtype) for o in outs[len(outs) - far_out :]),
        in_specs=[pl.BlockSpec(memory_space=pltpu.SMEM)] * smem
        + [pl.BlockSpec()] * near
        + [pl.BlockSpec(memory_space=pltpu.HBM)] * far,
        out_specs=tuple([pl.BlockSpec()] * (len(outs) - far_out))
        + tuple([pl.BlockSpec(memory_space=pltpu.HBM)] * far_out),
        scratch_shapes=list(scratch),
        compiler_params=pltpu.CompilerParams(vmem_limit_bytes=grant),
        cost_estimate=pl.CostEstimate(flops=flops, bytes_accessed=nbytes, transcendentals=trans),
    )


def sds(shape, dtype=BF16):
    return jax.ShapeDtypeStruct(shape, dtype)


def run(kernel, outs, args, far=0, **kw):
    shapes = [sds(a.shape, a.dtype) for a in args]
    near = len(args) - far
    args = list(args[:near]) + [
        pltpu.with_memory_space_constraint(a, pltpu.HBM) for a in args[near:]
    ]
    return call(kernel, outs, shapes, far=far, **kw)(*args)


def dot(a, b, ca, cb):
    return lax.dot_general(a, b, (((ca,), (cb,)), ((), ())), preferred_element_type=F32)


def copies_of(pairs, sems):
    made = [pltpu.make_async_copy(src, dst, sems.at[i]) for i, (src, dst) in enumerate(pairs)]
    for copy in made:
        copy.start()
    return made


def join(wq, wk, wv, wo, x_far, dy_far, gain_far, n_out, dy_out, w_far, w, x, gain, sems):
    parts = ((wq, 0, 384), (wk, 384, 512), (wv, 512, 640), (wo, 640, 1024))
    pairs = [(src, w.at[:, a:b]) for src, a, b in parts]
    pairs += [(gain_far, gain), (x_far, x), (dy_far, dy_out)]
    copies = copies_of(pairs, sems)
    for copy in copies[:4]:
        copy.wait()
    out_copy = pltpu.make_async_copy(w, w_far, sems.at[7])
    out_copy.start()
    copies[4].wait()
    copies[5].wait()
    xf = x[...].astype(F32)
    inv = lax.rsqrt(jnp.mean(xf * xf, axis=1, keepdims=True) + EPS)
    n_out[...] = (xf * inv * gain[...].reshape(1, -1).astype(F32)).astype(BF16)
    copies[6].wait()
    out_copy.wait()


def split(total, q_out, k_out, v_out, o_out, q, k, v, o, sems):
    parts = ((q, q_out, 0, 384), (k, k_out, 384, 512), (v, v_out, 512, 640), (o, o_out, 640, 1024))
    copies = copies_of([(total.at[:, a:b], part) for part, _, a, b in parts], sems)
    sent = []
    for i, (part, dst, _, _) in enumerate(parts):
        copies[i].wait()
        copy = pltpu.make_async_copy(part, dst, sems.at[4 + i])
        copy.start()
        sent.append(copy)
    for copy in sent:
        copy.wait()


def lay_out(n, dy, out_far, out, sems):
    sent = []
    for q in range(Q):
        cols = [slice((Q * z + q) * 160, (Q * z + q + 1) * 160) for z in range(Z)]
        row = jnp.concatenate([n[:, c] for c in cols] + [dy[:, c] for c in cols], axis=1)
        for t in range(T):
            out[q * T + t] = row
        part = pl.ds(q * T, T)
        copy = pltpu.make_async_copy(out.at[part], out_far.at[part], sems.at[q])
        copy.start()
        sent.append(copy)
    for copy in sent:
        copy.wait()


def project(g_ref, tokens, w_far, keep, send, w, total, sems):
    halves = (slice(0, 640), slice(640, 1280))
    parts = ((0, 384, 0), (384, 640, 0), (640, 1024, 1280))
    copies = copies_of([(w_far.at[rows], w.at[rows]) for rows in halves], sems)
    copies[0].wait()
    for first, last, at in parts:
        total[:, first:last] = dot(tokens[:, at : at + 640], w[halves[0], first:last], 1, 0)
    copies[1].wait()
    for first, last, at in parts:
        part = dot(tokens[:, at + 640 : at + 1280], w[halves[1], first:last], 1, 0)
        total[:, first:last] += part
    for xh in range(2):
        for core, out in ((0, keep), (1, send)):
            rows = pl.ds(pl.multiple_of((g_ref[0] ^ (2 * xh + core)) * 128, 128), 128)
            out[xh] = total[rows, :].astype(BF16)


def add(keep, pair, out):
    out[...] = (keep[1].astype(F32) + pair[1].astype(F32)).astype(BF16)


def heads_to_rows(a):
    return jnp.concatenate([a[:, HD * h : HD * (h + 1)] for h in range(QPER)], axis=0)


def rows_to_heads(a):
    n = a.shape[0] // QPER
    return jnp.concatenate([a[n * h : n * (h + 1), :] for h in range(QPER)], axis=1)


def attend(limit_ref, mine, pair, far, cosf, sinf, kc, vc, out):
    raw = mine[0].astype(F32) + pair[0].astype(F32) + far[...].astype(F32)
    cos, sin = cosf[...], sinf[...]

    def rotate(v):
        return v * cos + jnp.roll(v, HD // 2, axis=1) * sin

    def unrotate(v):
        return v * cos - jnp.roll(v, HD // 2, axis=1) * sin

    q = jnp.concatenate(
        [rotate(raw[:, HD * h : HD * (h + 1)]) for h in range(QPER)], axis=0
    ).astype(BF16)
    k = rotate(raw[:, 384:512]).astype(BF16)
    v = raw[:, 512:640].astype(BF16)
    da = heads_to_rows(raw[:, 640:].astype(BF16))
    rows, slots, new = q.shape[0], kc.shape[0], k.shape[0]
    scale = 1.0 / math.sqrt(HD)
    old_s = dot(q, kc[...], 1, 1) * scale
    new_s = dot(q, k, 1, 1) * scale
    old_ok = lax.broadcasted_iota(jnp.int32, (rows, slots), 1) < limit_ref[0]
    token = lax.rem(lax.broadcasted_iota(jnp.int32, (rows, new), 0), new)
    new_ok = lax.broadcasted_iota(jnp.int32, (rows, new), 1) <= token
    old_s = jnp.where(old_ok, old_s, -jnp.inf)
    new_s = jnp.where(new_ok, new_s, -jnp.inf)
    top = jnp.maximum(
        jnp.max(old_s, axis=1, keepdims=True), jnp.max(new_s, axis=1, keepdims=True)
    )
    old_e = jnp.exp(old_s - top)
    new_e = jnp.exp(new_s - top)
    total = jnp.sum(old_e, axis=1, keepdims=True) + jnp.sum(new_e, axis=1, keepdims=True)
    share = 1.0 / total
    old_w = old_e * share
    new_w = new_e * share
    new_p = new_w.astype(BF16)
    att = (dot(old_w.astype(BF16), vc[...], 1, 0) + dot(new_p, v, 1, 0)).astype(BF16)
    out[:, 640:] = rows_to_heads(att)

    delta = jnp.sum(da.astype(F32) * att.astype(F32), axis=1, keepdims=True)
    old_ds = (old_w * (dot(da, vc[...], 1, 1) - delta) * scale).astype(BF16)
    new_ds = (new_w * (dot(da, v, 1, 1) - delta) * scale).astype(BF16)
    dq = dot(old_ds, kc[...], 1, 0) + dot(new_ds, k, 1, 0)
    dk = dot(new_ds, q, 0, 0)
    dv = dot(new_p, da, 0, 0)
    for h in range(QPER):
        out[:, HD * h : HD * (h + 1)] = unrotate(dq[128 * h : 128 * (h + 1), :]).astype(BF16)
    out[:, 384:512] = unrotate(dk).astype(BF16)
    out[:, 512:640] = dv.astype(BF16)


def gather_rows(g_ref, cots, cot):
    for d, block in enumerate(cots):
        rows = pl.ds(pl.multiple_of((g_ref[0] ^ d) * 128, 128), 128)
        cot[rows, :] = block[:, : cot.shape[1]]


def weight_grad(g_ref, tokens, c0, c1, c2, c3, cot_out, grad_far, grad, cot, sems):
    gather_rows(g_ref, (c0, c1, c2, c3), cot)
    cot_out[...] = cot[:, :640]
    sent = []
    for r in range(5):
        cols = slice(256 * r, 256 * (r + 1))
        late = slice(1280 + 256 * r, 1280 + 256 * (r + 1))
        grad[cols, :640] = dot(tokens[:, cols], cot[:, :640], 0, 0).astype(BF16)
        grad[cols, 640:] = dot(tokens[:, late], cot[:, 640:], 0, 0).astype(BF16)
        copy = pltpu.make_async_copy(grad.at[cols], grad_far.at[cols], sems.at[r])
        copy.start()
        sent.append(copy)
    for copy in sent:
        copy.wait()


def input_grad(tokens, cot, w_far, out_far, w, out, sems):
    sent = []
    halves = (slice(0, 256), slice(256, 1280))
    copies = copies_of([(w_far.at[rows, :640], w.at[rows]) for rows in halves], sems)
    sums = []
    for r in range(5):
        cols = slice(256 * r, 256 * (r + 1))
        if r < 2:
            copies[r].wait()
        dn = dot(cot[...], w[cols, :], 1, 1)
        sums.append(jnp.sum(dn * tokens[:, cols].astype(F32), axis=0, keepdims=True))
        dn = dn.astype(BF16)
        for b in range(Q * T):
            out[b, :, cols] = dn[16 * b : 16 * (b + 1), :]
        copy = pltpu.make_async_copy(out.at[:, :, cols], out_far.at[:, :, cols], sems.at[6 + r])
        copy.start()
        sent.append(copy)
    total = jnp.concatenate(sums, axis=1)
    total = jnp.concatenate([total[:, 160 * z : 160 * (z + 1)] for z in range(Z)], axis=0)
    high = total.astype(BF16)
    low = (total - high.astype(F32)).astype(BF16)
    both = jnp.concatenate([high, low], axis=0)
    zero = jnp.zeros((16, 108), BF16)
    for t in range(T):
        tile = jnp.concatenate([both[:, 20 * t : 20 * (t + 1)], zero], axis=1)
        for q in range(Q):
            out[q * T + t, :, 1280:] = tile
    last = pltpu.make_async_copy(out.at[:, :, 1280:], out_far.at[:, :, 1280:], sems.at[11])
    last.start()
    for copy in sent + [last]:
        copy.wait()


def normalize(x, xhat, inv):
    xf = x[...].astype(F32)
    scale = lax.rsqrt(jnp.mean(xf * xf, axis=1, keepdims=True) + EPS)
    xhat[...] = xf * scale
    inv[...] = jnp.broadcast_to(scale, (16, 128))


def gain_sum(g_ref, parts, gain_out):
    tile = parts[g_ref[0], 0, :, 1280:].astype(F32)
    for t in range(1, T):
        tile = tile + parts[g_ref[0], t, :, 1280:].astype(F32)
    gain_out[...] = tile[:8, :] + tile[8:, :]


def finish(parts, xhat, inv, dy, gain, out):
    sums = []
    for q in range(Q):
        a = parts[q, 0, :, :1280].astype(F32)
        for t in range(1, T):
            a = a + parts[q, t, :, :1280].astype(F32)
        sums.append(a)
    dn = jnp.concatenate(
        [sums[q][:, 160 * z : 160 * (z + 1)] for z in range(Z) for q in range(Q)], axis=1
    )
    scaled = dn * gain[...].reshape(1, -1).astype(F32)
    mean = jnp.mean(scaled * xhat[...], axis=1, keepdims=True)
    out[...] = (dy[...].astype(F32) + inv[:, :1] * (scaled - xhat[...] * mean)).astype(BF16)


def tie(*arrays):
    return lax.optimization_barrier(arrays)


def swap(a, axis):
    return lax.ppermute(a, axis, [(0, 1), (1, 0)])


def body(x, dy, gain, wq, wk, wv, wo, kc, vc, slab_start, prefix_len):
    z = lax.axis_index("z").astype(jnp.int32)
    gs = lax.axis_index(QUARTER).astype(jnp.int32).reshape(1)
    kc, vc = kc.reshape(1024, HD), vc.reshape(1024, HD)

    n_own, dy_own, w_own = run(
        join,
        [sds((16, 5120)), sds((16, 5120)), sds((160, 1024))],
        (wq, wk, wv, wo.T, x, dy, gain),
        far=7,
        far_out=1,
        scratch=[
            pltpu.VMEM((160, 1024), BF16),
            pltpu.VMEM((16, 5120), BF16),
            pltpu.VMEM((5120,), BF16),
            pltpu.SemaphoreType.DMA((8,)),
        ],
        nbytes=1 << 20,
    )
    w = lax.all_gather(w_own, "z", axis=0, tiled=True)
    (sent,) = run(
        lay_out,
        [sds((Q * T, 16, 2560))],
        (n_own, dy_own),
        far_out=1,
        scratch=[pltpu.VMEM((Q * T, 16, 2560), BF16), pltpu.SemaphoreType.DMA((Q,))],
        nbytes=3 << 20,
    )
    tokens = lax.all_to_all(sent, PLANE, 0, 0).reshape(512, 2560)

    positions = (slab_start[0] + jnp.arange(128, dtype=jnp.int32)).astype(F32)
    freqs = jnp.power(F32(THETA), jnp.arange(HD // 2, dtype=F32) * (-2.0 / HD))
    phase = positions[:, None] * freqs[None, :]
    cos, sin = jnp.cos(phase), jnp.sin(phase)
    cosf = jnp.concatenate([cos, cos], axis=1)
    sinf = jnp.concatenate([-sin, sin], axis=1)
    tokens, cosf, sinf = tie(tokens, cosf, sinf)

    keep, send = run(
        project,
        [sds((2, 128, 1024)), sds((2, 128, 1024))],
        (gs, tokens, w),
        smem=1,
        far=1,
        scratch=[
            pltpu.VMEM((1280, 1024), BF16),
            pltpu.VMEM((512, 1024), F32),
            pltpu.SemaphoreType.DMA((2,)),
        ],
        flops=2 * 512 * 1280 * 1024,
        nbytes=7 << 20,
    )
    pair = swap(send, "c")
    (passed,) = run(add, [sds((128, 1024))], (keep, pair), nbytes=1 << 20)
    far = swap(passed, "xh")
    (cot,) = run(
        attend,
        [sds((128, 1024))],
        (prefix_len, keep, pair, far, cosf, sinf, kc, vc),
        smem=1,
        flops=10 * 384 * 1152 * HD,
        nbytes=4 << 20,
        trans=384 * 1152,
    )
    across = swap(cot, "xh")
    cots = (cot, swap(cot, "c"), across, swap(across, "c"))
    cot4, grads = run(
        weight_grad,
        [sds((512, 640)), sds((1280, 1024))],
        (gs, tokens, *cots),
        smem=1,
        far_out=1,
        scratch=[
            pltpu.VMEM((1280, 1024), BF16),
            pltpu.VMEM((512, 1024), BF16),
            pltpu.SemaphoreType.DMA((5,)),
        ],
        flops=2 * 512 * 1280 * 1024,
        nbytes=8 << 20,
    )
    total = lax.psum_scatter(grads, "z", scatter_dimension=0, tiled=True)
    (dn,) = run(
        input_grad,
        [sds((Q * T, 16, 1408))],
        (tokens, cot4, w),
        far=1,
        far_out=1,
        scratch=[
            pltpu.VMEM((1280, 640), BF16),
            pltpu.VMEM((Q * T, 16, 1408), BF16),
            pltpu.SemaphoreType.DMA((12,)),
        ],
        flops=2 * 512 * 1280 * 640,
        nbytes=7 << 20,
    )
    x_late, dn = tie(x, dn)
    dn_parts = lax.all_to_all(dn, PLANE, 0, 0)
    xhat, inv = run(normalize, [sds((16, 5120), F32), sds((16, 128), F32)], (x_late,), flops=LONG)
    dn_parts = dn_parts.reshape(Q, T, 16, 1408)
    (gain_z,) = run(gain_sum, [sds((8, 128), F32)], (gs, dn_parts), smem=1)
    (d_input,) = run(
        finish,
        [sds((16, 5120))],
        (dn_parts, xhat, inv, dy, gain),
        nbytes=2 << 20,
    )
    pieces = lax.all_to_all(gain_z.reshape(Z, 1, 128), "z", 0, 0)
    gq, gk, gv, go = run(
        split,
        [sds((160, 384)), sds((160, 128)), sds((160, 128)), sds((160, 384))],
        (total,),
        far=1,
        far_out=4,
        scratch=[
            pltpu.VMEM((160, 384), BF16),
            pltpu.VMEM((160, 128), BF16),
            pltpu.VMEM((160, 128), BF16),
            pltpu.VMEM((160, 384), BF16),
            pltpu.SemaphoreType.DMA((8,)),
        ],
        nbytes=2 << 20,
    )
    pieces, gq = tie(pieces, gq)
    own = (z * Q + lax.axis_index(QUARTER)) * T + lax.axis_index(HEADS)
    own_gain = lax.dynamic_slice_in_dim(gain, own * 20, 20).astype(F32)
    grad_gain = jnp.sum(pieces, axis=(0, 1))[:20] / own_gain

    return d_input, gq, gk, gv, go.T, grad_gain


def solution(mesh):
    fine = Mesh(mesh.devices.reshape(8, 2, 2, 4, 2), ("z", "xh", "c", "y", "xl"))
    dp = ("z", "xh", "c")
    both = dp + HEADS
    return jax.shard_map(
        body,
        mesh=fine,
        in_specs=(
            P(both, None),
            P(both, None),
            P(),
            P(dp, HEADS),
            P(dp, HEADS),
            P(dp, HEADS),
            P(HEADS, dp),
            P(dp, None, HEADS),
            P(dp, None, HEADS),
            P(dp),
            P(dp),
        ),
        out_specs=(
            P(both, None),
            P(dp, HEADS),
            P(dp, HEADS),
            P(dp, HEADS),
            P(HEADS, dp),
            P(both),
        ),
        check_vma=False,
    )
```

```python
import math

import jax
import jax.numpy as jnp
from jax import lax
from jax.experimental import pallas as pl
from jax.experimental.pallas import tpu as pltpu
from jax.sharding import Mesh
from jax.sharding import PartitionSpec as P

HD = 128
QPER = 3
EPS = 1e-06
THETA = 1000000.0

Z = 8
Q = 4
T = 8
QUARTER = ("xh", "c")
HEADS = ("y", "xl")
PLANE = ("xh", "c", "y", "xl")
VMEM = 16 * 1024 * 1024
LONG = 1 << 35
F32 = jnp.float32
BF16 = jnp.bfloat16


def call(
    kernel, outs, shapes, smem=0, far=0, far_out=0, scratch=(), flops=0, nbytes=0, trans=0, grant=VMEM
):
    near = len(shapes) - smem - far
    return pl.pallas_call(
        kernel,
        out_shape=tuple(outs[: len(outs) - far_out])
        + tuple(pltpu.HBM(o.shape, o.dtype) for o in outs[len(outs) - far_out :]),
        in_specs=[pl.BlockSpec(memory_space=pltpu.SMEM)] * smem
        + [pl.BlockSpec()] * near
        + [pl.BlockSpec(memory_space=pltpu.HBM)] * far,
        out_specs=tuple([pl.BlockSpec()] * (len(outs) - far_out))
        + tuple([pl.BlockSpec(memory_space=pltpu.HBM)] * far_out),
        scratch_shapes=list(scratch),
        compiler_params=pltpu.CompilerParams(vmem_limit_bytes=grant),
        cost_estimate=pl.CostEstimate(flops=flops, bytes_accessed=nbytes, transcendentals=trans),
    )


def sds(shape, dtype=BF16):
    return jax.ShapeDtypeStruct(shape, dtype)


def run(kernel, outs, args, far=0, **kw):
    shapes = [sds(a.shape, a.dtype) for a in args]
    near = len(args) - far
    args = list(args[:near]) + [
        pltpu.with_memory_space_constraint(a, pltpu.HBM) for a in args[near:]
    ]
    return call(kernel, outs, shapes, far=far, **kw)(*args)


def dot(a, b, ca, cb):
    return lax.dot_general(a, b, (((ca,), (cb,)), ((), ())), preferred_element_type=F32)


def copies_of(pairs, sems):
    made = [pltpu.make_async_copy(src, dst, sems.at[i]) for i, (src, dst) in enumerate(pairs)]
    for copy in made:
        copy.start()
    return made


def prepare(
    wq, wk, wv, wo, x_far, dy_far, gain_far, w_far, out_far, w, x, dy, gain, out, sems
):
    parts = ((wq, 0, 384), (wk, 384, 512), (wv, 512, 640), (wo, 640, 1024))
    pairs = [(src, w.at[:, a:b]) for src, a, b in parts]
    pairs += [(x_far, x), (gain_far, gain), (dy_far, dy)]
    copies = copies_of(pairs, sems)
    for copy in copies[:4]:
        copy.wait()
    sent = [pltpu.make_async_copy(w, w_far, sems.at[7])]
    sent[0].start()
    for copy in copies[4:]:
        copy.wait()
    xf = x[...].astype(F32)
    inv = lax.rsqrt(jnp.mean(xf * xf, axis=1, keepdims=True) + EPS)
    n = (xf * inv * gain[...].reshape(1, -1).astype(F32)).astype(BF16)
    for q in range(Q):
        cols = [slice((Q * z + q) * 160, (Q * z + q + 1) * 160) for z in range(Z)]
        row = jnp.concatenate([n[:, c] for c in cols] + [dy[:, c] for c in cols], axis=1)
        for t in range(T):
            out[q * T + t] = row
        part = pl.ds(q * T, T)
        copy = pltpu.make_async_copy(out.at[part], out_far.at[part], sems.at[8 + q])
        copy.start()
        sent.append(copy)
    for copy in sent:
        copy.wait()


def split(total, q_out, k_out, v_out, o_out, q, k, v, o, sems):
    parts = ((q, q_out, 0, 384), (k, k_out, 384, 512), (v, v_out, 512, 640), (o, o_out, 640, 1024))
    copies = copies_of([(total.at[:, a:b], part) for part, _, a, b in parts], sems)
    sent = []
    for i, (part, dst, _, _) in enumerate(parts):
        copies[i].wait()
        copy = pltpu.make_async_copy(part, dst, sems.at[4 + i])
        copy.start()
        sent.append(copy)
    for copy in sent:
        copy.wait()


def project(g_ref, tokens, w_far, keep, send, w, total, sems):
    halves = (slice(0, 640), slice(640, 1280))
    parts = ((0, 384, 0), (384, 640, 0), (640, 1024, 1280))
    copies = copies_of([(w_far.at[rows], w.at[rows]) for rows in halves], sems)
    copies[0].wait()
    for first, last, at in parts:
        total[:, first:last] = dot(tokens[:, at : at + 640], w[halves[0], first:last], 1, 0)
    copies[1].wait()
    for first, last, at in parts:
        part = dot(tokens[:, at + 640 : at + 1280], w[halves[1], first:last], 1, 0)
        total[:, first:last] += part
    for xh in range(2):
        for core, out in ((0, keep), (1, send)):
            rows = pl.ds(pl.multiple_of((g_ref[0] ^ (2 * xh + core)) * 128, 128), 128)
            out[xh] = total[rows, :].astype(BF16)


def add(keep, pair, out):
    out[...] = (keep[1].astype(F32) + pair[1].astype(F32)).astype(BF16)


def heads_to_rows(a):
    return jnp.concatenate([a[:, HD * h : HD * (h + 1)] for h in range(QPER)], axis=0)


def rows_to_heads(a):
    n = a.shape[0] // QPER
    return jnp.concatenate([a[n * h : n * (h + 1), :] for h in range(QPER)], axis=1)


def attend(limit_ref, mine, pair, far, cosf, sinf, kc, vc, out):
    raw = mine[0].astype(F32) + pair[0].astype(F32) + far[...].astype(F32)
    cos, sin = cosf[...], sinf[...]

    def rotate(v):
        return v * cos + jnp.roll(v, HD // 2, axis=1) * sin

    def unrotate(v):
        return v * cos - jnp.roll(v, HD // 2, axis=1) * sin

    q = jnp.concatenate(
        [rotate(raw[:, HD * h : HD * (h + 1)]) for h in range(QPER)], axis=0
    ).astype(BF16)
    k = rotate(raw[:, 384:512]).astype(BF16)
    v = raw[:, 512:640].astype(BF16)
    da = heads_to_rows(raw[:, 640:].astype(BF16))
    rows, slots, new = q.shape[0], kc.shape[0], k.shape[0]
    scale = 1.0 / math.sqrt(HD)
    old_s = dot(q, kc[...], 1, 1) * scale
    new_s = dot(q, k, 1, 1) * scale
    old_ok = lax.broadcasted_iota(jnp.int32, (rows, slots), 1) < limit_ref[0]
    token = lax.rem(lax.broadcasted_iota(jnp.int32, (rows, new), 0), new)
    new_ok = lax.broadcasted_iota(jnp.int32, (rows, new), 1) <= token
    old_s = jnp.where(old_ok, old_s, -jnp.inf)
    new_s = jnp.where(new_ok, new_s, -jnp.inf)
    top = jnp.maximum(
        jnp.max(old_s, axis=1, keepdims=True), jnp.max(new_s, axis=1, keepdims=True)
    )
    old_e = jnp.exp(old_s - top)
    new_e = jnp.exp(new_s - top)
    total = jnp.sum(old_e, axis=1, keepdims=True) + jnp.sum(new_e, axis=1, keepdims=True)
    share = 1.0 / total
    old_w = old_e * share
    new_w = new_e * share
    new_p = new_w.astype(BF16)
    att = (dot(old_w.astype(BF16), vc[...], 1, 0) + dot(new_p, v, 1, 0)).astype(BF16)
    out[:, 640:] = rows_to_heads(att)

    delta = jnp.sum(da.astype(F32) * att.astype(F32), axis=1, keepdims=True)
    old_ds = (old_w * (dot(da, vc[...], 1, 1) - delta) * scale).astype(BF16)
    new_ds = (new_w * (dot(da, v, 1, 1) - delta) * scale).astype(BF16)
    dq = dot(old_ds, kc[...], 1, 0) + dot(new_ds, k, 1, 0)
    dk = dot(new_ds, q, 0, 0)
    dv = dot(new_p, da, 0, 0)
    for h in range(QPER):
        out[:, HD * h : HD * (h + 1)] = unrotate(dq[128 * h : 128 * (h + 1), :]).astype(BF16)
    out[:, 384:512] = unrotate(dk).astype(BF16)
    out[:, 512:640] = dv.astype(BF16)


def gather_rows(g_ref, cots, cot):
    for d, block in enumerate(cots):
        rows = pl.ds(pl.multiple_of((g_ref[0] ^ d) * 128, 128), 128)
        cot[rows, :] = block[:, : cot.shape[1]]


def weight_grad_near(g_ref, tokens, c0, c1, out, cot):
    core = lax.rem(g_ref[0], 2)
    cot[pl.ds(pl.multiple_of(core * 128, 128), 128), :] = c0[...]
    cot[pl.ds(pl.multiple_of((1 - core) * 128, 128), 128), :] = c1[...]
    rows = pl.ds(pl.multiple_of((g_ref[0] - core) * 128, 256), 256)
    for r in range(5):
        cols = slice(256 * r, 256 * (r + 1))
        late = slice(1280 + 256 * r, 1280 + 256 * (r + 1))
        out[cols, :640] = dot(tokens[rows, cols], cot[:, :640], 0, 0).astype(BF16)
        out[cols, 640:] = dot(tokens[rows, late], cot[:, 640:], 0, 0).astype(BF16)


def weight_grad(g_ref, tokens, near, c0, c1, c2, c3, cot_out, grad_far, grad, cot, sems):
    gather_rows(g_ref, (c0, c1, c2, c3), cot)
    cot_out[...] = cot[:, :640]
    first = g_ref[0] - lax.rem(g_ref[0], 2)
    rows = pl.ds(pl.multiple_of((2 - first) * 128, 256), 256)
    sent = []
    for r in range(5):
        cols = slice(256 * r, 256 * (r + 1))
        late = slice(1280 + 256 * r, 1280 + 256 * (r + 1))
        part = dot(tokens[rows, cols], cot[rows, :640], 0, 0)
        grad[cols, :640] = (near[cols, :640].astype(F32) + part).astype(BF16)
        part = dot(tokens[rows, late], cot[rows, 640:], 0, 0)
        grad[cols, 640:] = (near[cols, 640:].astype(F32) + part).astype(BF16)
        copy = pltpu.make_async_copy(grad.at[cols], grad_far.at[cols], sems.at[r])
        copy.start()
        sent.append(copy)
    for copy in sent:
        copy.wait()


def input_grad(tokens, cot, w_far, out_far, w, out, sems):
    sent = []
    halves = (slice(0, 256), slice(256, 1280))
    copies = copies_of([(w_far.at[rows, :640], w.at[rows]) for rows in halves], sems)
    sums = []
    for r in range(5):
        cols = slice(256 * r, 256 * (r + 1))
        if r < 2:
            copies[r].wait()
        dn = dot(cot[...], w[cols, :], 1, 1)
        sums.append(jnp.sum(dn * tokens[:, cols].astype(F32), axis=0, keepdims=True))
        dn = dn.astype(BF16)
        for b in range(Q * T):
            out[b, :, cols] = dn[16 * b : 16 * (b + 1), :]
        copy = pltpu.make_async_copy(out.at[:, :, cols], out_far.at[:, :, cols], sems.at[6 + r])
        copy.start()
        sent.append(copy)
    total = jnp.concatenate(sums, axis=1)
    total = jnp.concatenate([total[:, 160 * z : 160 * (z + 1)] for z in range(Z)], axis=0)
    high = total.astype(BF16)
    low = (total - high.astype(F32)).astype(BF16)
    both = jnp.concatenate([high, low], axis=0)
    zero = jnp.zeros((16, 108), BF16)
    for t in range(T):
        tile = jnp.concatenate([both[:, 20 * t : 20 * (t + 1)], zero], axis=1)
        for q in range(Q):
            out[q * T + t, :, 1280:] = tile
    last = pltpu.make_async_copy(out.at[:, :, 1280:], out_far.at[:, :, 1280:], sems.at[11])
    last.start()
    for copy in sent + [last]:
        copy.wait()


def normalize(x, xhat, inv):
    xf = x[...].astype(F32)
    scale = lax.rsqrt(jnp.mean(xf * xf, axis=1, keepdims=True) + EPS)
    xhat[...] = xf * scale
    inv[...] = jnp.broadcast_to(scale, (16, 128))


def gain_sum(g_ref, parts, gain_out):
    tile = parts[g_ref[0], 0, :, 1280:].astype(F32)
    for t in range(1, T):
        tile = tile + parts[g_ref[0], t, :, 1280:].astype(F32)
    gain_out[...] = tile[:8, :] + tile[8:, :]


def finish(parts, xhat, inv, dy, gain, out):
    sums = []
    for q in range(Q):
        a = parts[q, 0, :, :1280].astype(F32)
        for t in range(1, T):
            a = a + parts[q, t, :, :1280].astype(F32)
        sums.append(a)
    dn = jnp.concatenate(
        [sums[q][:, 160 * z : 160 * (z + 1)] for z in range(Z) for q in range(Q)], axis=1
    )
    scaled = dn * gain[...].reshape(1, -1).astype(F32)
    mean = jnp.mean(scaled * xhat[...], axis=1, keepdims=True)
    out[...] = (dy[...].astype(F32) + inv[:, :1] * (scaled - xhat[...] * mean)).astype(BF16)


def tie(*arrays):
    return lax.optimization_barrier(arrays)


def swap(a, axis):
    return lax.ppermute(a, axis, [(0, 1), (1, 0)])


def body(x, dy, gain, wq, wk, wv, wo, kc, vc, slab_start, prefix_len):
    z = lax.axis_index("z").astype(jnp.int32)
    gs = lax.axis_index(QUARTER).astype(jnp.int32).reshape(1)
    kc, vc = kc.reshape(1024, HD), vc.reshape(1024, HD)

    w_own, sent = run(
        prepare,
        [sds((160, 1024)), sds((Q * T, 16, 2560))],
        (wq, wk, wv, wo.T, x, dy, gain),
        far=7,
        far_out=2,
        scratch=[
            pltpu.VMEM((160, 1024), BF16),
            pltpu.VMEM((16, 5120), BF16),
            pltpu.VMEM((16, 5120), BF16),
            pltpu.VMEM((5120,), BF16),
            pltpu.VMEM((Q * T, 16, 2560), BF16),
            pltpu.SemaphoreType.DMA((8 + Q,)),
        ],
        nbytes=4 << 20,
    )
    w = lax.all_gather(w_own, "z", axis=0, tiled=True)
    tokens = lax.all_to_all(sent, PLANE, 0, 0).reshape(512, 2560)

    positions = (slab_start[0] + jnp.arange(128, dtype=jnp.int32)).astype(F32)
    freqs = jnp.power(F32(THETA), jnp.arange(HD // 2, dtype=F32) * (-2.0 / HD))
    phase = positions[:, None] * freqs[None, :]
    cos, sin = jnp.cos(phase), jnp.sin(phase)
    cosf = jnp.concatenate([cos, cos], axis=1)
    sinf = jnp.concatenate([-sin, sin], axis=1)
    tokens, cosf, sinf = tie(tokens, cosf, sinf)

    keep, send = run(
        project,
        [sds((2, 128, 1024)), sds((2, 128, 1024))],
        (gs, tokens, w),
        smem=1,
        far=1,
        scratch=[
            pltpu.VMEM((1280, 1024), BF16),
            pltpu.VMEM((512, 1024), F32),
            pltpu.SemaphoreType.DMA((2,)),
        ],
        flops=2 * 512 * 1280 * 1024,
        nbytes=7 << 20,
    )
    pair = swap(send, "c")
    (passed,) = run(add, [sds((128, 1024))], (keep, pair), nbytes=1 << 20)
    far = swap(passed, "xh")
    (cot,) = run(
        attend,
        [sds((128, 1024))],
        (prefix_len, keep, pair, far, cosf, sinf, kc, vc),
        smem=1,
        flops=10 * 384 * 1152 * HD,
        nbytes=4 << 20,
        trans=384 * 1152,
    )
    across = swap(cot, "xh")
    cots = (cot, swap(cot, "c"), across, swap(across, "c"))
    (near,) = run(
        weight_grad_near,
        [sds((1280, 1024))],
        (gs, tokens, cots[0], cots[1]),
        smem=1,
        scratch=[pltpu.VMEM((256, 1024), BF16)],
        flops=512 * 1280 * 1024,
        nbytes=6 << 20,
    )
    cot4, grads = run(
        weight_grad,
        [sds((512, 640)), sds((1280, 1024))],
        (gs, tokens, near, *cots),
        smem=1,
        far_out=1,
        scratch=[
            pltpu.VMEM((1280, 1024), BF16),
            pltpu.VMEM((512, 1024), BF16),
            pltpu.SemaphoreType.DMA((5,)),
        ],
        flops=512 * 1280 * 1024,
        nbytes=8 << 20,
    )
    total = lax.psum_scatter(grads, "z", scatter_dimension=0, tiled=True)
    (dn,) = run(
        input_grad,
        [sds((Q * T, 16, 1408))],
        (tokens, cot4, w),
        far=1,
        far_out=1,
        scratch=[
            pltpu.VMEM((1280, 640), BF16),
            pltpu.VMEM((Q * T, 16, 1408), BF16),
            pltpu.SemaphoreType.DMA((12,)),
        ],
        flops=2 * 512 * 1280 * 640,
        nbytes=7 << 20,
    )
    x_late, dn = tie(x, dn)
    dn_parts = lax.all_to_all(dn, PLANE, 0, 0)
    xhat, inv = run(normalize, [sds((16, 5120), F32), sds((16, 128), F32)], (x_late,), flops=LONG)
    dn_parts = dn_parts.reshape(Q, T, 16, 1408)
    (gain_z,) = run(gain_sum, [sds((8, 128), F32)], (gs, dn_parts), smem=1)
    (d_input,) = run(
        finish,
        [sds((16, 5120))],
        (dn_parts, xhat, inv, dy, gain),
        nbytes=2 << 20,
    )
    pieces = lax.all_to_all(gain_z.reshape(Z, 1, 128), "z", 0, 0)
    gq, gk, gv, go = run(
        split,
        [sds((160, 384)), sds((160, 128)), sds((160, 128)), sds((160, 384))],
        (total,),
        far=1,
        far_out=4,
        scratch=[
            pltpu.VMEM((160, 384), BF16),
            pltpu.VMEM((160, 128), BF16),
            pltpu.VMEM((160, 128), BF16),
            pltpu.VMEM((160, 384), BF16),
            pltpu.SemaphoreType.DMA((8,)),
        ],
        nbytes=2 << 20,
    )
    pieces, gq = tie(pieces, gq)
    own = (z * Q + lax.axis_index(QUARTER)) * T + lax.axis_index(HEADS)
    own_gain = lax.dynamic_slice_in_dim(gain, own * 20, 20).astype(F32)
    grad_gain = jnp.sum(pieces, axis=(0, 1))[:20] / own_gain

    return d_input, gq, gk, gv, go.T, grad_gain


def solution(mesh):
    fine = Mesh(mesh.devices.reshape(8, 2, 2, 4, 2), ("z", "xh", "c", "y", "xl"))
    dp = ("z", "xh", "c")
    both = dp + HEADS
    return jax.shard_map(
        body,
        mesh=fine,
        in_specs=(
            P(both, None),
            P(both, None),
            P(),
            P(dp, HEADS),
            P(dp, HEADS),
            P(dp, HEADS),
            P(HEADS, dp),
            P(dp, None, HEADS),
            P(dp, None, HEADS),
            P(dp),
            P(dp),
        ),
        out_specs=(
            P(both, None),
            P(dp, HEADS),
            P(dp, HEADS),
            P(dp, HEADS),
            P(HEADS, dp),
            P(both),
        ),
        check_vma=False,
    )
```

```python
import math

import jax
import jax.numpy as jnp
from jax import lax
from jax.experimental import pallas as pl
from jax.experimental.pallas import tpu as pltpu
from jax.sharding import Mesh
from jax.sharding import PartitionSpec as P

HD = 128
QPER = 3
EPS = 1e-06
THETA = 1000000.0

Z = 8
Q = 4
T = 8
QUARTER = ("xh", "c")
HEADS = ("y", "xl")
PLANE = ("xh", "c", "y", "xl")
VMEM = 16 * 1024 * 1024
LONG = 1 << 35
F32 = jnp.float32
BF16 = jnp.bfloat16


def call(
    kernel, outs, shapes, smem=0, far=0, far_out=0, scratch=(), flops=0, nbytes=0, trans=0, grant=VMEM
):
    near = len(shapes) - smem - far
    return pl.pallas_call(
        kernel,
        out_shape=tuple(outs[: len(outs) - far_out])
        + tuple(pltpu.HBM(o.shape, o.dtype) for o in outs[len(outs) - far_out :]),
        in_specs=[pl.BlockSpec(memory_space=pltpu.SMEM)] * smem
        + [pl.BlockSpec()] * near
        + [pl.BlockSpec(memory_space=pltpu.HBM)] * far,
        out_specs=tuple([pl.BlockSpec()] * (len(outs) - far_out))
        + tuple([pl.BlockSpec(memory_space=pltpu.HBM)] * far_out),
        scratch_shapes=list(scratch),
        compiler_params=pltpu.CompilerParams(vmem_limit_bytes=grant),
        cost_estimate=pl.CostEstimate(flops=flops, bytes_accessed=nbytes, transcendentals=trans),
    )


def sds(shape, dtype=BF16):
    return jax.ShapeDtypeStruct(shape, dtype)


def run(kernel, outs, args, far=0, **kw):
    shapes = [sds(a.shape, a.dtype) for a in args]
    near = len(args) - far
    args = list(args[:near]) + [
        pltpu.with_memory_space_constraint(a, pltpu.HBM) for a in args[near:]
    ]
    return call(kernel, outs, shapes, far=far, **kw)(*args)


def dot(a, b, ca, cb):
    return lax.dot_general(a, b, (((ca,), (cb,)), ((), ())), preferred_element_type=F32)


def copies_of(pairs, sems):
    made = [pltpu.make_async_copy(src, dst, sems.at[i]) for i, (src, dst) in enumerate(pairs)]
    for copy in made:
        copy.start()
    return made


def prepare(
    wq, wk, wv, wo, x_far, dy_far, gain_far, w_far, out_far, w, x, dy, gain, out, sems
):
    parts = ((wq, 0, 384), (wk, 384, 512), (wv, 512, 640), (wo, 640, 1024))
    pairs = [(x_far, x), (gain_far, gain), (dy_far, dy)]
    pairs += [(src, w.at[:, a:b]) for src, a, b in parts]
    copies = copies_of(pairs, sems)
    copies[0].wait()
    xf = x[...].astype(F32)
    inv = lax.rsqrt(jnp.mean(xf * xf, axis=1, keepdims=True) + EPS)
    copies[1].wait()
    n = (xf * inv * gain[...].reshape(1, -1).astype(F32)).astype(BF16)
    for copy in copies[2:]:
        copy.wait()
    sent = [pltpu.make_async_copy(w, w_far, sems.at[7])]
    sent[0].start()
    for q in range(Q):
        cols = [slice((Q * z + q) * 160, (Q * z + q + 1) * 160) for z in range(Z)]
        row = jnp.concatenate([n[:, c] for c in cols] + [dy[:, c] for c in cols], axis=1)
        for t in range(T):
            out[q * T + t] = row
        part = pl.ds(q * T, T)
        copy = pltpu.make_async_copy(out.at[part], out_far.at[part], sems.at[8 + q])
        copy.start()
        sent.append(copy)
    for copy in sent:
        copy.wait()


def split(total, q_out, k_out, v_out, o_out, q, k, v, o, sems):
    parts = ((q, q_out, 0, 384), (k, k_out, 384, 512), (v, v_out, 512, 640), (o, o_out, 640, 1024))
    copies = copies_of([(total.at[:, a:b], part) for part, _, a, b in parts], sems)
    sent = []
    for i, (part, dst, _, _) in enumerate(parts):
        copies[i].wait()
        copy = pltpu.make_async_copy(part, dst, sems.at[4 + i])
        copy.start()
        sent.append(copy)
    for copy in sent:
        copy.wait()


def project(g_ref, tokens, w_far, keep, send, w, held, sems):
    pieces = [slice(160 * z, 160 * (z + 1)) for z in range(Z)]
    for copy in copies_of([(w_far.at[rows], w.at[rows]) for rows in pieces], sems):
        copy.wait()
    for first, last, at in ((0, 384, 0), (384, 640, 0), (640, 1024, 1280)):
        part = dot(tokens[:, at : at + 1280], w[:, first:last], 1, 0).astype(BF16)
        for g in range(Q):
            held[g_ref[0] ^ g, :, first:last] = part[128 * g : 128 * (g + 1), :]
    for xh in range(2):
        keep[xh] = held[2 * xh]
        send[xh] = held[2 * xh + 1]


def add(keep, pair, out):
    out[...] = (keep[1].astype(F32) + pair[1].astype(F32)).astype(BF16)


def heads_to_rows(a):
    return jnp.concatenate([a[:, HD * h : HD * (h + 1)] for h in range(QPER)], axis=0)


def rows_to_heads(a):
    n = a.shape[0] // QPER
    return jnp.concatenate([a[n * h : n * (h + 1), :] for h in range(QPER)], axis=1)


def attend(limit_ref, mine, pair, far, cosf, sinf, kc, vc, out):
    raw = mine[0].astype(F32) + pair[0].astype(F32) + far[...].astype(F32)
    cos, sin = cosf[...], sinf[...]

    def rotate(v):
        return v * cos + jnp.roll(v, HD // 2, axis=1) * sin

    def unrotate(v):
        return v * cos - jnp.roll(v, HD // 2, axis=1) * sin

    q = jnp.concatenate(
        [rotate(raw[:, HD * h : HD * (h + 1)]) for h in range(QPER)], axis=0
    ).astype(BF16)
    k = rotate(raw[:, 384:512]).astype(BF16)
    v = raw[:, 512:640].astype(BF16)
    da = heads_to_rows(raw[:, 640:].astype(BF16))
    rows, slots, new = q.shape[0], kc.shape[0], k.shape[0]
    scale = 1.0 / math.sqrt(HD)
    old_s = dot(q, kc[...], 1, 1) * scale
    new_s = dot(q, k, 1, 1) * scale
    old_ok = lax.broadcasted_iota(jnp.int32, (rows, slots), 1) < limit_ref[0]
    token = lax.rem(lax.broadcasted_iota(jnp.int32, (rows, new), 0), new)
    new_ok = lax.broadcasted_iota(jnp.int32, (rows, new), 1) <= token
    old_s = jnp.where(old_ok, old_s, -jnp.inf)
    new_s = jnp.where(new_ok, new_s, -jnp.inf)
    top = jnp.maximum(
        jnp.max(old_s, axis=1, keepdims=True), jnp.max(new_s, axis=1, keepdims=True)
    )
    old_e = jnp.exp(old_s - top)
    new_e = jnp.exp(new_s - top)
    total = jnp.sum(old_e, axis=1, keepdims=True) + jnp.sum(new_e, axis=1, keepdims=True)
    share = 1.0 / total
    old_w = old_e * share
    new_w = new_e * share
    new_p = new_w.astype(BF16)
    att = (dot(old_w.astype(BF16), vc[...], 1, 0) + dot(new_p, v, 1, 0)).astype(BF16)
    out[:, 640:] = rows_to_heads(att)

    delta = jnp.sum(da.astype(F32) * att.astype(F32), axis=1, keepdims=True)
    old_ds = (old_w * (dot(da, vc[...], 1, 1) - delta) * scale).astype(BF16)
    new_ds = (new_w * (dot(da, v, 1, 1) - delta) * scale).astype(BF16)
    dq = dot(old_ds, kc[...], 1, 0) + dot(new_ds, k, 1, 0)
    dk = dot(new_ds, q, 0, 0)
    dv = dot(new_p, da, 0, 0)
    for h in range(QPER):
        out[:, HD * h : HD * (h + 1)] = unrotate(dq[128 * h : 128 * (h + 1), :]).astype(BF16)
    out[:, 384:512] = unrotate(dk).astype(BF16)
    out[:, 512:640] = dv.astype(BF16)


def gather_rows(g_ref, cots, cot):
    for d, block in enumerate(cots):
        rows = pl.ds(pl.multiple_of((g_ref[0] ^ d) * 128, 128), 128)
        cot[rows, :] = block[:, : cot.shape[1]]


def weight_grad_near(g_ref, tokens, c0, c1, out, cot):
    core = lax.rem(g_ref[0], 2)
    cot[pl.ds(pl.multiple_of(core * 128, 128), 128), :] = c0[...]
    cot[pl.ds(pl.multiple_of((1 - core) * 128, 128), 128), :] = c1[...]
    rows = pl.ds(pl.multiple_of((g_ref[0] - core) * 128, 256), 256)
    for r in range(5):
        cols = slice(256 * r, 256 * (r + 1))
        late = slice(1280 + 256 * r, 1280 + 256 * (r + 1))
        out[cols, :640] = dot(tokens[rows, cols], cot[:, :640], 0, 0).astype(BF16)
        out[cols, 640:] = dot(tokens[rows, late], cot[:, 640:], 0, 0).astype(BF16)


def weight_grad(g_ref, tokens, near, c0, c1, c2, c3, cot_out, grad_far, grad, cot, sems):
    gather_rows(g_ref, (c0, c1, c2, c3), cot)
    cot_out[...] = cot[:, :640]
    first = g_ref[0] - lax.rem(g_ref[0], 2)
    rows = pl.ds(pl.multiple_of((2 - first) * 128, 256), 256)
    sent = []
    for r in range(5):
        cols = slice(256 * r, 256 * (r + 1))
        late = slice(1280 + 256 * r, 1280 + 256 * (r + 1))
        part = dot(tokens[rows, cols], cot[rows, :640], 0, 0)
        grad[cols, :640] = (near[cols, :640].astype(F32) + part).astype(BF16)
        part = dot(tokens[rows, late], cot[rows, 640:], 0, 0)
        grad[cols, 640:] = (near[cols, 640:].astype(F32) + part).astype(BF16)
        copy = pltpu.make_async_copy(grad.at[cols], grad_far.at[cols], sems.at[r])
        copy.start()
        sent.append(copy)
    for copy in sent:
        copy.wait()


def input_grad(tokens, cot, w_far, out_far, w, out, sems):
    sent = []
    halves = (slice(0, 256), slice(256, 1280))
    copies = copies_of([(w_far.at[rows, :640], w.at[rows]) for rows in halves], sems)
    sums = []
    for r in range(5):
        cols = slice(256 * r, 256 * (r + 1))
        if r < 2:
            copies[r].wait()
        dn = dot(cot[...], w[cols, :], 1, 1)
        sums.append(jnp.sum(dn * tokens[:, cols].astype(F32), axis=0, keepdims=True))
        dn = dn.astype(BF16)
        for b in range(Q * T):
            out[b, :, cols] = dn[16 * b : 16 * (b + 1), :]
        copy = pltpu.make_async_copy(out.at[:, :, cols], out_far.at[:, :, cols], sems.at[6 + r])
        copy.start()
        sent.append(copy)
    total = jnp.concatenate(sums, axis=1)
    total = jnp.concatenate([total[:, 160 * z : 160 * (z + 1)] for z in range(Z)], axis=0)
    high = total.astype(BF16)
    low = (total - high.astype(F32)).astype(BF16)
    both = jnp.concatenate([high, low], axis=0)
    zero = jnp.zeros((16, 108), BF16)
    for t in range(T):
        tile = jnp.concatenate([both[:, 20 * t : 20 * (t + 1)], zero], axis=1)
        for q in range(Q):
            out[q * T + t, :, 1280:] = tile
    last = pltpu.make_async_copy(out.at[:, :, 1280:], out_far.at[:, :, 1280:], sems.at[11])
    last.start()
    for copy in sent + [last]:
        copy.wait()


def normalize(x, xhat, inv):
    xf = x[...].astype(F32)
    scale = lax.rsqrt(jnp.mean(xf * xf, axis=1, keepdims=True) + EPS)
    xhat[...] = xf * scale
    inv[...] = jnp.broadcast_to(scale, (16, 128))


def gain_sum(g_ref, parts, gain_out):
    tile = parts[g_ref[0], 0, :, 1280:].astype(F32)
    for t in range(1, T):
        tile = tile + parts[g_ref[0], t, :, 1280:].astype(F32)
    gain_out[...] = tile[:8, :] + tile[8:, :]


def finish(parts, xhat, inv, dy, gain, out):
    sums = []
    for q in range(Q):
        a = parts[q, 0, :, :1280].astype(F32)
        for t in range(1, T):
            a = a + parts[q, t, :, :1280].astype(F32)
        sums.append(a)
    dn = jnp.concatenate(
        [sums[q][:, 160 * z : 160 * (z + 1)] for z in range(Z) for q in range(Q)], axis=1
    )
    scaled = dn * gain[...].reshape(1, -1).astype(F32)
    mean = jnp.mean(scaled * xhat[...], axis=1, keepdims=True)
    out[...] = (dy[...].astype(F32) + inv[:, :1] * (scaled - xhat[...] * mean)).astype(BF16)


def tie(*arrays):
    return lax.optimization_barrier(arrays)


def swap(a, axis):
    return lax.ppermute(a, axis, [(0, 1), (1, 0)])


def body(x, dy, gain, wq, wk, wv, wo, kc, vc, slab_start, prefix_len):
    z = lax.axis_index("z").astype(jnp.int32)
    gs = lax.axis_index(QUARTER).astype(jnp.int32).reshape(1)
    kc, vc = kc.reshape(1024, HD), vc.reshape(1024, HD)

    w_own, sent = run(
        prepare,
        [sds((160, 1024)), sds((Q * T, 16, 2560))],
        (wq, wk, wv, wo.T, x, dy, gain),
        far=7,
        far_out=2,
        scratch=[
            pltpu.VMEM((160, 1024), BF16),
            pltpu.VMEM((16, 5120), BF16),
            pltpu.VMEM((16, 5120), BF16),
            pltpu.VMEM((5120,), BF16),
            pltpu.VMEM((Q * T, 16, 2560), BF16),
            pltpu.SemaphoreType.DMA((8 + Q,)),
        ],
        nbytes=4 << 20,
    )
    w = lax.all_gather(w_own, "z", axis=0, tiled=True)
    tokens = lax.all_to_all(sent, PLANE, 0, 0).reshape(512, 2560)

    positions = (slab_start[0] + jnp.arange(128, dtype=jnp.int32)).astype(F32)
    freqs = jnp.power(F32(THETA), jnp.arange(HD // 2, dtype=F32) * (-2.0 / HD))
    phase = positions[:, None] * freqs[None, :]
    cos, sin = jnp.cos(phase), jnp.sin(phase)
    cosf = jnp.concatenate([cos, cos], axis=1)
    sinf = jnp.concatenate([-sin, sin], axis=1)
    tokens, cosf, sinf = tie(tokens, cosf, sinf)

    keep, send = run(
        project,
        [sds((2, 128, 1024)), sds((2, 128, 1024))],
        (gs, tokens, w),
        smem=1,
        far=1,
        scratch=[
            pltpu.VMEM((1280, 1024), BF16),
            pltpu.VMEM((Q, 128, 1024), BF16),
            pltpu.SemaphoreType.DMA((Z,)),
        ],
        flops=2 * 512 * 1280 * 1024,
        nbytes=7 << 20,
    )
    pair = swap(send, "c")
    (passed,) = run(add, [sds((128, 1024))], (keep, pair), nbytes=1 << 20)
    far = swap(passed, "xh")
    (cot,) = run(
        attend,
        [sds((128, 1024))],
        (prefix_len, keep, pair, far, cosf, sinf, kc, vc),
        smem=1,
        flops=10 * 384 * 1152 * HD,
        nbytes=4 << 20,
        trans=384 * 1152,
    )
    across = swap(cot, "xh")
    cots = (cot, swap(cot, "c"), across, swap(across, "c"))
    (near,) = run(
        weight_grad_near,
        [sds((1280, 1024))],
        (gs, tokens, cots[0], cots[1]),
        smem=1,
        scratch=[pltpu.VMEM((256, 1024), BF16)],
        flops=512 * 1280 * 1024,
        nbytes=6 << 20,
    )
    cot4, grads = run(
        weight_grad,
        [sds((512, 640)), sds((1280, 1024))],
        (gs, tokens, near, *cots),
        smem=1,
        far_out=1,
        scratch=[
            pltpu.VMEM((1280, 1024), BF16),
            pltpu.VMEM((512, 1024), BF16),
            pltpu.SemaphoreType.DMA((5,)),
        ],
        flops=512 * 1280 * 1024,
        nbytes=8 << 20,
    )
    total = lax.psum_scatter(grads, "z", scatter_dimension=0, tiled=True)
    (dn,) = run(
        input_grad,
        [sds((Q * T, 16, 1408))],
        (tokens, cot4, w),
        far=1,
        far_out=1,
        scratch=[
            pltpu.VMEM((1280, 640), BF16),
            pltpu.VMEM((Q * T, 16, 1408), BF16),
            pltpu.SemaphoreType.DMA((12,)),
        ],
        flops=2 * 512 * 1280 * 640,
        nbytes=7 << 20,
    )
    x_late, dn = tie(x, dn)
    dn_parts = lax.all_to_all(dn, PLANE, 0, 0)
    xhat, inv = run(normalize, [sds((16, 5120), F32), sds((16, 128), F32)], (x_late,), flops=LONG)
    dn_parts = dn_parts.reshape(Q, T, 16, 1408)
    (gain_z,) = run(gain_sum, [sds((8, 128), F32)], (gs, dn_parts), smem=1)
    (d_input,) = run(
        finish,
        [sds((16, 5120))],
        (dn_parts, xhat, inv, dy, gain),
        nbytes=2 << 20,
    )
    pieces = lax.all_to_all(gain_z.reshape(Z, 1, 128), "z", 0, 0)
    gq, gk, gv, go = run(
        split,
        [sds((160, 384)), sds((160, 128)), sds((160, 128)), sds((160, 384))],
        (total,),
        far=1,
        far_out=4,
        scratch=[
            pltpu.VMEM((160, 384), BF16),
            pltpu.VMEM((160, 128), BF16),
            pltpu.VMEM((160, 128), BF16),
            pltpu.VMEM((160, 384), BF16),
            pltpu.SemaphoreType.DMA((8,)),
        ],
        nbytes=2 << 20,
    )
    pieces, gq = tie(pieces, gq)
    own = (z * Q + lax.axis_index(QUARTER)) * T + lax.axis_index(HEADS)
    own_gain = lax.dynamic_slice_in_dim(gain, own * 20, 20).astype(F32)
    grad_gain = jnp.sum(pieces, axis=(0, 1))[:20] / own_gain

    return d_input, gq, gk, gv, go.T, grad_gain


def solution(mesh):
    fine = Mesh(mesh.devices.reshape(8, 2, 2, 4, 2), ("z", "xh", "c", "y", "xl"))
    dp = ("z", "xh", "c")
    both = dp + HEADS
    return jax.shard_map(
        body,
        mesh=fine,
        in_specs=(
            P(both, None),
            P(both, None),
            P(),
            P(dp, HEADS),
            P(dp, HEADS),
            P(dp, HEADS),
            P(HEADS, dp),
            P(dp, None, HEADS),
            P(dp, None, HEADS),
            P(dp),
            P(dp),
        ),
        out_specs=(
            P(both, None),
            P(dp, HEADS),
            P(dp, HEADS),
            P(dp, HEADS),
            P(HEADS, dp),
            P(both),
        ),
        check_vma=False,
    )
```
